32 devices in a mesh: section: 4 (over x, core), tensor: 8 (over z, y).
Axes of the slice: x: 2, y: 2, z: 4, core: 2. Of those that a mesh axis runs over, the one named last changes fastest.
Arguments:
- hidden: bfloat16 [4, 256, 8192], P('section', 'tensor'), may hold values from -60 to 60
- norm_gain: float32 [8192], replicated, may hold values from 0.1 to 1.9
- lengths: int32 [4], P('section'), may hold values from 64 to 256
- query_param: float32 [8192, 4096], P(('section', 'tensor')), may hold values from -1.3258252 to 1.3258252
- query_grad: float32 [8192, 4096], P(('section', 'tensor')), may hold values from -0.006 to 0.006
- query_moment: float32 [8192, 4096], P(('section', 'tensor')), may hold values from -0.006 to 0.006
- query_second: float32 [8192, 4096], P(('section', 'tensor')), may hold values from 1e-07 to 1e-05
- keyval_param: float32 [8192, 1024], P(('section', 'tensor')), may hold values from -0.06629126 to 0.06629126
- keyval_gradient: float32 [8192, 1024], P(('section', 'tensor')), may hold values from -0.006 to 0.006
- keyval_first_moment: float32 [8192, 1024], P(('section', 'tensor')), may hold values from -0.006 to 0.006
- keyval_second_moment: float32 [8192, 1024], P(('section', 'tensor')), may hold values from 1e-07 to 1e-05
- output_param: float32 [8192, 4096], P(('section', 'tensor')), may hold values from -0.25 to 0.25
- output_grad: float32 [8192, 4096], P(('section', 'tensor')), may hold values from -0.006 to 0.006
- output_moment: float32 [8192, 4096], P(('section', 'tensor')), may hold values from -0.006 to 0.006
- output_second: float32 [8192, 4096], P(('section', 'tensor')), may hold values from 1e-07 to 1e-05
Outputs:
- mixed: bfloat16 [4, 256, 8192], P('section', 'tensor')
The draws below stay inside these ranges and needn't reach their ends.
All inputs are finite; a program needn't handle non-finite values.
Results may differ from the reference program's by a relative error of at most 0.017.
Values may be sent and summed in bfloat16 or wider, within the bound.
A program may use at most 128 MiB of HBM per device.

```python
import math
import jax
import jax.numpy as jnp
from jax import lax

MODEL_DIMENSION = 8192
QUERY_HEADS_LOCAL = 32
KEYVAL_HEADS = 4
HEAD_DIMENSION = 128
PROMPT_LENGTH = 256
PROMPTS = 4
N_TENSOR = 8


def joint_weights(key):
    base_key = jax.random.fold_in(key, 7)
    key_query, keyval_random_key = jax.random.split(base_key, 2)
    query_part = jnp.clip(jax.random.normal(key_query, (MODEL_DIMENSION, QUERY_HEADS_LOCAL * HEAD_DIMENSION), jnp.float32), -6.0, 6.0) * MODEL_DIMENSION ** (-0.5)
    keyval_piece_slice = jnp.clip(jax.random.normal(keyval_random_key, (MODEL_DIMENSION, 2 * KEYVAL_HEADS * HEAD_DIMENSION), jnp.float32), -6.0, 6.0) * MODEL_DIMENSION ** (-0.5)
    return (query_part, keyval_piece_slice)


def draw_query_param(key, part):
    return joint_weights(key)[0]


def draw_keyval_param(key, part):
    return joint_weights(key)[1]


def draw_hidden(key, part):
    key_rows, key_columns_part, key_normal = jax.random.split(jax.random.fold_in(key, 11), 3)
    row_scale = jnp.exp(jax.random.uniform(key_rows, (PROMPTS, PROMPT_LENGTH, 1), jnp.float32, -1.204, 1.098))
    col_scale = jnp.exp(jax.random.uniform(key_columns_part, (1, 1, MODEL_DIMENSION), jnp.float32, -1.204, 1.098))
    normal_part = jnp.clip(jax.random.normal(key_normal, (PROMPTS, PROMPT_LENGTH, MODEL_DIMENSION), jnp.float32), -4.0, 4.0)
    return (normal_part * row_scale * col_scale).astype(jnp.bfloat16)


def draw_lengths(key, part):
    key_values, key_index = jax.random.split(jax.random.fold_in(key, 3))
    values = jax.random.randint(key_values, (PROMPTS,), PROMPT_LENGTH // 4, PROMPT_LENGTH + 1)
    full_index = jax.random.randint(key_index, (), 0, PROMPTS)
    return jnp.where(jnp.arange(PROMPTS) == full_index, PROMPT_LENGTH, values).astype(jnp.int32)


def block_scale(stream_key, extent, cuts, smallest, high):
    def one(axis_at, blocks):
        draws = jax.random.uniform(jax.random.fold_in(jax.random.fold_in(stream_key, 6), axis_at), (blocks,), jnp.float32, smallest / len(cuts), high / len(cuts))
        return jnp.repeat(jnp.exp(draws), extent[axis_at] // blocks).reshape((-1,) + (1,) * (len(extent) - axis_at - 1))

    factor_of = one(*cuts[0])
    for cut in cuts[1:]:
        factor_of = factor_of * one(*cut)
    return factor_of


def noise(own_key, dims, scale, limit, cuts=(), kind=jnp.bfloat16):
    level = block_scale(own_key, dims, cuts, -0.22, 0.18) if cuts else 1.0
    array = jax.random.normal(own_key, dims, jnp.float32) * scale * level
    return jnp.minimum(jnp.maximum(array, -limit), limit).astype(kind)


def setup_inputs(seed: int = 0) -> dict:
    key_of = jax.random.split(jax.random.key(seed), 16)
    hidden = draw_hidden(jax.random.fold_in(key_of[15], 71), 0)
    norm_gain = jnp.clip(1.0 + 0.18 * jax.random.normal(key_of[1], (MODEL_DIMENSION,), jnp.float32), 0.1, 1.9)
    lengths = draw_lengths(jax.random.fold_in(key_of[15], 71), 0)
    query_param = draw_query_param(jax.random.fold_in(key_of[15], 71), 0)
    query_grad = noise(key_of[4], (MODEL_DIMENSION, QUERY_HEADS_LOCAL * HEAD_DIMENSION), 0.001, 0.006, ((0, 32),), jnp.float32)
    query_moment = noise(key_of[5], (MODEL_DIMENSION, QUERY_HEADS_LOCAL * HEAD_DIMENSION), 0.001, 0.006, ((0, 32),), jnp.float32)
    query_second = jnp.clip(jnp.exp(math.log(9.999999747378752e-06) - 4.6051701 * jax.random.uniform(key_of[6], (MODEL_DIMENSION, QUERY_HEADS_LOCAL * HEAD_DIMENSION), jnp.float32) ** block_scale(key_of[6], (MODEL_DIMENSION, QUERY_HEADS_LOCAL * HEAD_DIMENSION), ((0, 32),), -0.2, 0.2)), 1.0000000116860974e-07, 9.999999747378752e-06)
    keyval_param = draw_keyval_param(jax.random.fold_in(key_of[15], 71), 0)
    keyval_gradient = noise(key_of[8], (MODEL_DIMENSION, 2 * KEYVAL_HEADS * HEAD_DIMENSION), 0.001, 0.006, ((0, 32),), jnp.float32)
    keyval_first_moment = noise(key_of[9], (MODEL_DIMENSION, 2 * KEYVAL_HEADS * HEAD_DIMENSION), 0.001, 0.006, ((0, 32),), jnp.float32)
    keyval_second_moment = jnp.clip(jnp.exp(math.log(9.999999747378752e-06) - 4.6051701 * jax.random.uniform(key_of[10], (MODEL_DIMENSION, 2 * KEYVAL_HEADS * HEAD_DIMENSION), jnp.float32) ** block_scale(key_of[10], (MODEL_DIMENSION, 2 * KEYVAL_HEADS * HEAD_DIMENSION), ((0, 32),), -0.2, 0.2)), 1.0000000116860974e-07, 9.999999747378752e-06)
    output_param = noise(key_of[11], (MODEL_DIMENSION, QUERY_HEADS_LOCAL * HEAD_DIMENSION), (4 * HEAD_DIMENSION) ** -0.5, 0.25, ((0, 32),), jnp.float32)
    output_grad = noise(key_of[12], (MODEL_DIMENSION, QUERY_HEADS_LOCAL * HEAD_DIMENSION), 0.001, 0.006, ((0, 32),), jnp.float32)
    output_moment = noise(key_of[13], (MODEL_DIMENSION, QUERY_HEADS_LOCAL * HEAD_DIMENSION), 0.001, 0.006, ((0, 32),), jnp.float32)
    output_second = jnp.clip(jnp.exp(math.log(9.999999747378752e-06) - 4.6051701 * jax.random.uniform(key_of[14], (MODEL_DIMENSION, QUERY_HEADS_LOCAL * HEAD_DIMENSION), jnp.float32) ** block_scale(key_of[14], (MODEL_DIMENSION, QUERY_HEADS_LOCAL * HEAD_DIMENSION), ((0, 32),), -0.2, 0.2)), 1.0000000116860974e-07, 9.999999747378752e-06)
    return {"hidden": hidden, "norm_gain": norm_gain, "lengths": lengths, "query_param": query_param, "query_grad": query_grad, "query_moment": query_moment, "query_second": query_second, "keyval_param": keyval_param, "keyval_gradient": keyval_gradient, "keyval_first_moment": keyval_first_moment, "keyval_second_moment": keyval_second_moment, "output_param": output_param, "output_grad": output_grad, "output_moment": output_moment, "output_second": output_second}


learn_rate = 0.015
beta_one = 0.5
beta_two = 0.9
adam_step = 1000.0
adam_eps = 1e-08
decay_rate = 0.1
norm_eps = 1e-06
rope_base = 1000000.0
masked_score = -1e+30

def adam_update(current, gradient, moment, second):
    moment_new = beta_one * moment + (1.0 - beta_one) * gradient
    second_new = beta_two * second + (1.0 - beta_two) * gradient * gradient
    corrected = moment_new / (1.0 - beta_one ** adam_step)
    denominator = jnp.sqrt(second_new / (1.0 - beta_two ** adam_step)) + adam_eps
    return (current - learn_rate * (corrected / denominator + decay_rate * current)).astype(jnp.bfloat16)

def normalize(hidden, norm_gain):
    values = hidden.astype(jnp.float32)
    factor = lax.rsqrt(lax.optimization_barrier(jnp.mean(values * values, axis=-1, keepdims=True)) + norm_eps)
    return (values * factor * norm_gain).astype(jnp.bfloat16)

def rotary_embed(values, token_positions):
    half_width = values.shape[-1] // 2
    frequency = rope_base ** (-jnp.arange(half_width, dtype=jnp.float32) * 2.0 / values.shape[-1])
    angles = token_positions.astype(jnp.float32)[:, None] * frequency[None, :]
    cosine_table = jnp.concatenate([jnp.cos(angles), jnp.cos(angles)], axis=-1)
    sine_table = jnp.concatenate([jnp.sin(angles), jnp.sin(angles)], axis=-1)
    first_half = values[..., :half_width]
    second_half = values[..., half_width:]
    rotated = jnp.concatenate([-second_half, first_half], axis=-1)
    return values * cosine_table + rotated * sine_table

def prompt_layer(normed, length, query_weight, keyval_matrix, output_weight):
    queries = jnp.dot(normed, query_weight, preferred_element_type=jnp.float32)
    keyval_outputs = jnp.dot(normed, keyval_matrix, preferred_element_type=jnp.float32)
    token_positions = jnp.arange(PROMPT_LENGTH)
    query_heads = rotary_embed(queries.reshape(PROMPT_LENGTH, QUERY_HEADS_LOCAL, HEAD_DIMENSION).transpose(1, 0, 2), token_positions).astype(jnp.bfloat16)
    key_head_rows = rotary_embed(keyval_outputs[:, :KEYVAL_HEADS * HEAD_DIMENSION].reshape(PROMPT_LENGTH, KEYVAL_HEADS, HEAD_DIMENSION).transpose(1, 0, 2), token_positions).astype(jnp.bfloat16)
    value_head_rows = keyval_outputs[:, KEYVAL_HEADS * HEAD_DIMENSION:].reshape(PROMPT_LENGTH, KEYVAL_HEADS, HEAD_DIMENSION).transpose(1, 0, 2).astype(jnp.bfloat16)
    group_width = QUERY_HEADS_LOCAL // KEYVAL_HEADS
    key_full = jnp.repeat(key_head_rows, group_width, axis=0)
    value_full = jnp.repeat(value_head_rows, group_width, axis=0)
    scores = jnp.einsum('hqd,hkd->hqk', query_heads.astype(jnp.float32), key_full.astype(jnp.float32)) / math.sqrt(HEAD_DIMENSION)
    allowed = (token_positions[None, :] <= token_positions[:, None]) & (token_positions[None, :] < length)
    scores = jnp.where(allowed[None], scores, masked_score)
    row_max = lax.optimization_barrier(jnp.max(scores, axis=-1, keepdims=True))
    exponent = jnp.exp(scores - row_max)
    attention = (exponent / lax.optimization_barrier(jnp.sum(exponent, axis=-1, keepdims=True))).astype(jnp.bfloat16)
    head_out = jnp.einsum('hqk,hkd->hqd', attention.astype(jnp.float32), value_full.astype(jnp.float32)).astype(jnp.bfloat16)
    head_out = head_out.transpose(1, 0, 2).reshape(PROMPT_LENGTH, QUERY_HEADS_LOCAL * HEAD_DIMENSION)
    group_cols = QUERY_HEADS_LOCAL * HEAD_DIMENSION // N_TENSOR
    head_groups = head_out.reshape(PROMPT_LENGTH, N_TENSOR, group_cols).transpose(1, 0, 2)
    weight_groups = output_weight.reshape(MODEL_DIMENSION, N_TENSOR, group_cols).transpose(1, 0, 2)

    def add_group(totals, sliced):
        head_part, weight_part = sliced
        partial_term = lax.dot_general(head_part, weight_part, (((1,), (1,)), ((), ())), preferred_element_type=jnp.float32)
        return (totals + partial_term.astype(jnp.bfloat16).astype(jnp.float32), None)
    summed, unused = lax.scan(add_group, jnp.zeros((PROMPT_LENGTH, MODEL_DIMENSION), jnp.float32), (head_groups, weight_groups))
    return summed.astype(jnp.bfloat16)

def reference(hidden, norm_gain, lengths, query_param, query_grad, query_moment, query_second, keyval_param, keyval_gradient, keyval_first_moment, keyval_second_moment, output_param, output_grad, output_moment, output_second):
    query_weight = adam_update(query_param, query_grad, query_moment, query_second)
    keyval_matrix = adam_update(keyval_param, keyval_gradient, keyval_first_moment, keyval_second_moment)
    output_weight = adam_update(output_param, output_grad, output_moment, output_second)
    normed = normalize(hidden, norm_gain)

    def one_prompt(packed):
        return prompt_layer(packed[0], packed[1], query_weight, keyval_matrix, output_weight)
    return lax.map(one_prompt, (normed, lengths))
```

```python
import math

import jax
import jax.numpy as jnp
from jax import lax
from jax.sharding import Mesh, PartitionSpec as P

QUERY_HEADS_LOCAL = 32
KEYVAL_HEADS = 4
HEAD_DIMENSION = 128


learn_rate = 0.015
beta_one = 0.5
beta_two = 0.9
adam_step = 1000.0
adam_eps = 1e-08
decay_rate = 0.1
norm_eps = 1e-06
rope_base = 1000000.0
masked_score = -1e30


def adam_update(current, gradient, moment, second):
    moment_new = beta_one * moment + (1.0 - beta_one) * gradient
    second_new = beta_two * second + (1.0 - beta_two) * gradient * gradient
    corrected = moment_new / (1.0 - beta_one**adam_step)
    denominator = jnp.sqrt(second_new / (1.0 - beta_two**adam_step)) + adam_eps
    return (current - learn_rate * (corrected / denominator + decay_rate * current)).astype(
        jnp.bfloat16
    )


def normalize(hidden, norm_gain):
    values = hidden.astype(jnp.float32)
    factor = lax.rsqrt(jnp.mean(values * values, axis=-1, keepdims=True) + norm_eps)
    return (values * factor * norm_gain).astype(jnp.bfloat16)


def rotary_embed(values, token_positions):
    half_width = values.shape[-1] // 2
    frequency = rope_base ** (-jnp.arange(half_width, dtype=jnp.float32) * 2.0 / values.shape[-1])
    angles = token_positions.astype(jnp.float32)[:, None] * frequency[None, :]
    cosine_table = jnp.concatenate([jnp.cos(angles), jnp.cos(angles)], axis=-1)
    sine_table = jnp.concatenate([jnp.sin(angles), jnp.sin(angles)], axis=-1)
    first_half = values[..., :half_width]
    second_half = values[..., half_width:]
    rotated = jnp.concatenate([-second_half, first_half], axis=-1)
    return values * cosine_table + rotated * sine_table


def on_device(
    hidden,
    norm_gain,
    lengths,
    query_param,
    query_grad,
    query_moment,
    query_second,
    keyval_param,
    keyval_gradient,
    keyval_first_moment,
    keyval_second_moment,
    output_param,
    output_grad,
    output_moment,
    output_second,
):
    sections = lax.axis_size("section")
    planes = lax.axis_size("plane")
    lanes = lax.axis_size("lane")
    members = sections * lanes
    group = ("section", "lane")
    rows = query_param.shape[0]
    head_columns = query_param.shape[1] // members
    heads_here = head_columns // HEAD_DIMENSION
    tokens_here, model_width = hidden.shape[1:]
    sequence = tokens_here * planes * lanes

    query_weight = adam_update(query_param, query_grad, query_moment, query_second)
    keyval_matrix = adam_update(
        keyval_param, keyval_gradient, keyval_first_moment, keyval_second_moment
    )
    output_weight = adam_update(output_param, output_grad, output_moment, output_second)

    spread_heads = jnp.repeat(
        keyval_matrix.reshape(rows, 2, KEYVAL_HEADS, HEAD_DIMENSION),
        members // KEYVAL_HEADS,
        axis=2,
    )
    spread_heads = spread_heads.transpose(2, 0, 1, 3).reshape(members, rows, 2 * HEAD_DIMENSION)
    query_pieces = query_weight.reshape(rows, members, head_columns).transpose(1, 0, 2)
    output_pieces = output_weight.reshape(rows, members, head_columns).transpose(1, 0, 2)
    query_rows = lax.all_to_all(query_pieces, group, 0, 0, tiled=True)
    keyval_rows = lax.all_to_all(spread_heads, group, 0, 0, tiled=True)
    output_rows = lax.all_to_all(output_pieces, group, 0, 0, tiled=True)
    query_rows = query_rows.reshape(members * rows, head_columns)
    keyval_rows = keyval_rows.reshape(members * rows, 2 * HEAD_DIMENSION)
    output_rows = output_rows.reshape(members * rows, head_columns)

    local_rows = normalize(hidden[0], norm_gain)
    features = local_rows.reshape(tokens_here, sections, planes, lanes * rows)
    features = features.transpose(2, 0, 1, 3).reshape(planes, tokens_here, members * rows)
    features = lax.all_to_all(features, "plane", 0, 0, tiled=True)
    normed = lax.all_gather(features, group, axis=0, tiled=True)
    normed = normed.reshape(sections * sequence, members * rows)

    partial = jnp.concatenate(
        [
            jnp.dot(normed, query_rows, preferred_element_type=jnp.float32).astype(jnp.bfloat16),
            jnp.dot(normed, keyval_rows, preferred_element_type=jnp.float32).astype(jnp.bfloat16),
        ],
        axis=1,
    ).reshape(sections, sequence, head_columns + 2 * HEAD_DIMENSION)
    partial = lax.all_to_all(partial, "plane", 0, 0, tiled=True)
    total = jnp.sum(partial.astype(jnp.float32), axis=0)

    order = jnp.arange(sequence).reshape(planes, lanes, tokens_here)
    token_positions = order.transpose(1, 0, 2).reshape(sequence)
    length = lax.dynamic_index_in_dim(
        lax.all_gather(lengths, "section", axis=0, tiled=True), lax.axis_index("plane"), 0, False
    )
    query_heads = rotary_embed(
        total[:, :head_columns].reshape(sequence, heads_here, HEAD_DIMENSION).transpose(1, 0, 2),
        token_positions,
    ).astype(jnp.bfloat16)
    key_head_rows = rotary_embed(
        total[:, head_columns : head_columns + HEAD_DIMENSION], token_positions
    ).astype(jnp.bfloat16)
    value_head_rows = total[:, head_columns + HEAD_DIMENSION :].astype(jnp.bfloat16)
    scores = jnp.einsum(
        "hqd,kd->hqk", query_heads, key_head_rows, preferred_element_type=jnp.float32
    ) / math.sqrt(HEAD_DIMENSION)
    allowed = (token_positions[None, :] <= token_positions[:, None]) & (
        token_positions[None, :] < length
    )
    scores = jnp.where(allowed[None], scores, masked_score)
    row_max = jnp.max(scores, axis=-1, keepdims=True)
    exponent = jnp.exp(scores - row_max)
    attention = (exponent / jnp.sum(exponent, axis=-1, keepdims=True)).astype(jnp.bfloat16)
    head_out = jnp.einsum(
        "hqk,kd->hqd", attention, value_head_rows, preferred_element_type=jnp.float32
    ).astype(jnp.bfloat16)
    head_out = head_out.transpose(1, 0, 2).reshape(sequence, head_columns)

    all_heads = lax.all_gather(head_out, "plane", axis=0, tiled=True)
    feature_part = lax.dot_general(
        all_heads, output_rows, (((1,), (1,)), ((), ())), preferred_element_type=jnp.float32
    ).astype(jnp.bfloat16)
    feature_part = feature_part.reshape(members, planes * tokens_here, members * rows)
    feature_part = lax.all_to_all(feature_part, group, 0, 0, tiled=True)
    summed = jnp.sum(feature_part.astype(jnp.float32), axis=0).astype(jnp.bfloat16)
    arrived = lax.all_to_all(
        summed.reshape(planes, tokens_here, members * rows), "plane", 0, 0, tiled=True
    )
    ordered = arrived.reshape(planes, tokens_here, sections, lanes * rows).transpose(1, 2, 0, 3)
    return ordered.reshape(1, tokens_here, model_width)


def solution(mesh):
    sections, tensors = mesh.shape["section"], mesh.shape["tensor"]
    lanes = tensors // sections
    grid = Mesh(
        mesh.devices.reshape(sections, tensors // lanes, lanes), ("section", "plane", "lane")
    )
    row_spec = P(("section", "plane", "lane"), None)
    token_spec = P("section", ("plane", "lane"), None)
    return jax.shard_map(
        on_device,
        mesh=grid,
        in_specs=(token_spec, P(), P("section")) + (row_spec,) * 12,
        out_specs=token_spec,
        check_vma=False,
    )
```

```python
import functools
import math

import jax
import jax.numpy as jnp
import numpy as np
from jax import lax
from jax.experimental import pallas as pl
from jax.experimental.pallas import tpu as pltpu
from jax.sharding import Mesh, PartitionSpec as P

QUERY_HEADS_LOCAL = 32
KEYVAL_HEADS = 4
HEAD_DIMENSION = 128


learn_rate = 0.015
beta_one = 0.5
beta_two = 0.9
adam_step = 1000.0
adam_eps = 1e-08
decay_rate = 0.1
norm_eps = 1e-06
rope_base = 1000000.0
masked_score = -1e30


def adam_update(current, gradient, moment, second):
    moment_new = beta_one * moment + (1.0 - beta_one) * gradient
    second_new = beta_two * second + (1.0 - beta_two) * gradient * gradient
    corrected = moment_new / (1.0 - beta_one**adam_step)
    denominator = jnp.sqrt(second_new / (1.0 - beta_two**adam_step)) + adam_eps
    return (current - learn_rate * (corrected / denominator + decay_rate * current)).astype(
        jnp.bfloat16
    )


def normalize(hidden, norm_gain):
    values = hidden.astype(jnp.float32)
    factor = lax.rsqrt(jnp.mean(values * values, axis=-1, keepdims=True) + norm_eps)
    return (values * factor * norm_gain).astype(jnp.bfloat16)


def rotary_embed(values, token_positions):
    half_width = values.shape[-1] // 2
    frequency = rope_base ** (-jnp.arange(half_width, dtype=jnp.float32) * 2.0 / values.shape[-1])
    angles = token_positions.astype(jnp.float32)[:, None] * frequency[None, :]
    cosine_table = jnp.concatenate([jnp.cos(angles), jnp.cos(angles)], axis=-1)
    sine_table = jnp.concatenate([jnp.sin(angles), jnp.sin(angles)], axis=-1)
    first_half = values[..., :half_width]
    second_half = values[..., half_width:]
    rotated = jnp.concatenate([-second_half, first_half], axis=-1)
    return values * cosine_table + rotated * sine_table


def on_device(
    hidden,
    norm_gain,
    lengths,
    query_param,
    query_grad,
    query_moment,
    query_second,
    keyval_param,
    keyval_gradient,
    keyval_first_moment,
    keyval_second_moment,
    output_param,
    output_grad,
    output_moment,
    output_second,
):
    sections = lax.axis_size("section")
    planes = lax.axis_size("plane")
    lanes = lax.axis_size("lane")
    members = sections * lanes
    group = ("section", "lane")
    rows = query_param.shape[0]
    head_columns = query_param.shape[1] // members
    heads_here = head_columns // HEAD_DIMENSION
    tokens_here, model_width = hidden.shape[1:]
    sequence = tokens_here * planes * lanes

    query_weight = adam_update(query_param, query_grad, query_moment, query_second)
    keyval_matrix = adam_update(
        keyval_param, keyval_gradient, keyval_first_moment, keyval_second_moment
    )
    output_weight = adam_update(output_param, output_grad, output_moment, output_second)

    spread_heads = jnp.repeat(
        keyval_matrix.reshape(rows, 2, KEYVAL_HEADS, HEAD_DIMENSION),
        members // KEYVAL_HEADS,
        axis=2,
    )
    spread_heads = spread_heads.transpose(2, 0, 1, 3).reshape(members, rows, 2 * HEAD_DIMENSION)
    query_pieces = query_weight.reshape(rows, members, head_columns).transpose(1, 0, 2)
    output_pieces = output_weight.reshape(rows, members, head_columns).transpose(1, 0, 2)
    query_rows = lax.all_to_all(query_pieces, group, 0, 0, tiled=True)
    keyval_rows = lax.all_to_all(spread_heads, group, 0, 0, tiled=True)
    output_rows = lax.all_to_all(output_pieces, group, 0, 0, tiled=True)
    query_rows = query_rows.reshape(members * rows, head_columns)
    keyval_rows = keyval_rows.reshape(members * rows, 2 * HEAD_DIMENSION)
    output_rows = output_rows.reshape(members * rows, head_columns)

    local_rows = normalize(hidden[0], norm_gain)
    features = local_rows.reshape(tokens_here, sections, planes, lanes * rows)
    features = features.transpose(2, 0, 1, 3).reshape(planes, tokens_here, members * rows)
    features = lax.all_to_all(features, "plane", 0, 0, tiled=True)
    normed = lax.all_gather(features, group, axis=0, tiled=True)
    normed = normed.reshape(sections * sequence, members * rows)

    partial = jnp.concatenate(
        [
            jnp.dot(normed, query_rows, preferred_element_type=jnp.float32).astype(jnp.bfloat16),
            jnp.dot(normed, keyval_rows, preferred_element_type=jnp.float32).astype(jnp.bfloat16),
        ],
        axis=1,
    ).reshape(sections, sequence, head_columns + 2 * HEAD_DIMENSION)
    partial = lax.all_to_all(partial, "plane", 0, 0, tiled=True)
    total = jnp.sum(partial.astype(jnp.float32), axis=0)

    order = jnp.arange(sequence).reshape(planes, lanes, tokens_here)
    token_positions = order.transpose(1, 0, 2).reshape(sequence)
    length = lax.dynamic_index_in_dim(
        lax.all_gather(lengths, "section", axis=0, tiled=True), lax.axis_index("plane"), 0, False
    )
    query_heads = rotary_embed(
        total[:, :head_columns].reshape(sequence, heads_here, HEAD_DIMENSION).transpose(1, 0, 2),
        token_positions,
    ).astype(jnp.bfloat16)
    key_head_rows = rotary_embed(
        total[:, head_columns : head_columns + HEAD_DIMENSION], token_positions
    ).astype(jnp.bfloat16)
    value_head_rows = total[:, head_columns + HEAD_DIMENSION :].astype(jnp.bfloat16)
    scores = jnp.einsum(
        "hqd,kd->hqk", query_heads, key_head_rows, preferred_element_type=jnp.float32
    ) / math.sqrt(HEAD_DIMENSION)
    allowed = (token_positions[None, :] <= token_positions[:, None]) & (
        token_positions[None, :] < length
    )
    scores = jnp.where(allowed[None], scores, masked_score)
    row_max = jnp.max(scores, axis=-1, keepdims=True)
    exponent = jnp.exp(scores - row_max)
    attention = (exponent / jnp.sum(exponent, axis=-1, keepdims=True)).astype(jnp.bfloat16)
    head_out = jnp.einsum(
        "hqk,kd->hqd", attention, value_head_rows, preferred_element_type=jnp.float32
    ).astype(jnp.bfloat16)
    head_out = head_out.transpose(1, 0, 2).reshape(sequence, head_columns)

    all_heads = lax.all_gather(head_out, "plane", axis=0, tiled=True)
    feature_part = lax.dot_general(
        all_heads, output_rows, (((1,), (1,)), ((), ())), preferred_element_type=jnp.float32
    ).astype(jnp.bfloat16)
    feature_part = feature_part.reshape(members, planes * tokens_here, members * rows)
    feature_part = lax.all_to_all(feature_part, group, 0, 0, tiled=True)
    summed = jnp.sum(feature_part.astype(jnp.float32), axis=0).astype(jnp.bfloat16)
    arrived = lax.all_to_all(
        summed.reshape(planes, tokens_here, members * rows), "plane", 0, 0, tiled=True
    )
    ordered = arrived.reshape(planes, tokens_here, sections, lanes * rows).transpose(1, 2, 0, 3)
    return ordered.reshape(1, tokens_here, model_width)


def rope_tables(positions):
    half_width = HEAD_DIMENSION // 2
    frequency = (
        rope_base ** (-np.arange(half_width, dtype=np.float64) * 2.0 / HEAD_DIMENSION)
    ).astype(np.float32)
    angles = positions.astype(np.float32)[:, None] * frequency[None, :]
    cosine, sine = np.cos(angles), np.sin(angles)
    return (
        np.concatenate([cosine, cosine], axis=-1).astype(np.float32),
        np.concatenate([-sine, sine], axis=-1).astype(np.float32),
    )


def block_kernel(
    sizes,
    hidden,
    norm_gain,
    length,
    cosine,
    sine,
    rows_at,
    columns_at,
    qp,
    qg,
    qm,
    qs,
    kp,
    kg,
    km,
    ks,
    op,
    og,
    om,
    os_,
    out,
    fetched,
    w_send,
    w_all,
    o_send,
    o_all,
    x_send,
    normed,
    part_send,
    part_recv,
    total,
    heads,
    pair_send,
    pair_recv,
    red_send,
    red_recv,
    z_send,
    z_recv,
    length_here,
    fetch_sem,
    local_sem,
    w_ssem,
    w_rsem,
    o_ssem,
    o_rsem,
    x_ssem,
    x_rsem,
    g_ssem,
    g_rsem,
    f_ssem,
    p_ssem,
    p_rsem,
    h_ssem,
    h_rsem,
    b_ssem,
    b_rsem,
    r_ssem,
    r_rsem,
    z_ssem,
    z_rsem,
    l_ssem,
    l_rsem,
):
    S, NP, L = sizes
    G = S * L
    half = S // 2
    s, p, l = lax.axis_index("section"), lax.axis_index("plane"), lax.axis_index("lane")
    j = s * L + l
    core = lax.rem(s, 2)
    pair = s // 2
    sibling = s + 1 - 2 * core
    rows = qp.shape[0]
    width = w_all.shape[2]
    hc = width - 2 * HEAD_DIMENSION
    tokens = hidden.shape[0]
    strip = L * rows
    seq = NP * tokens * L

    def member(m):
        return (m // L, p, lax.rem(m, L))

    def at_plane(q):
        return (s, q, l)

    def remote(src, dst, ssem, rsem, device):
        return pltpu.make_async_remote_copy(
            src_ref=src,
            dst_ref=dst,
            send_sem=ssem,
            recv_sem=rsem,
            device_id=device,
            device_id_type=pl.DeviceIdType.MESH,
        )

    same_core = []
    for da in range(half):
        for dl in range(L):
            sec = 2 * lax.rem(pair + da, half) + core
            lane = lax.rem(l + dl, L)
            same_core.append((sec, lane))
    others = same_core[1:]

    barrier = pltpu.get_barrier_semaphore()
    for d in range(1, G):
        pl.semaphore_signal(
            barrier, inc=1, device_id=member(lax.rem(j + d, G)), device_id_type=pl.DeviceIdType.MESH
        )
    for d in range(1, NP):
        pl.semaphore_signal(
            barrier,
            inc=1,
            device_id=at_plane(lax.rem(p + d, NP)),
            device_id_type=pl.DeviceIdType.MESH,
        )

    def fetch(refs, kv_refs, i, slot):
        dest = lax.rem(j + i, G)
        head = dest // (G // KEYVAL_HEADS)
        copies = []
        for a, ref in enumerate(refs):
            copies.append(
                pltpu.make_async_copy(
                    ref.at[:, pl.ds(pl.multiple_of(dest * hc, 128), hc)],
                    fetched.at[slot, a, :, pl.ds(0, hc)],
                    fetch_sem.at[slot, a, 0],
                )
            )
        for a, ref in enumerate(kv_refs):
            for part in range(2):
                copies.append(
                    pltpu.make_async_copy(
                        ref.at[
                            :,
                            pl.ds(
                                pl.multiple_of((part * KEYVAL_HEADS + head) * HEAD_DIMENSION, 128),
                                HEAD_DIMENSION,
                            ),
                        ],
                        fetched.at[slot, a, :, pl.ds(hc + part * HEAD_DIMENSION, HEAD_DIMENSION)],
                        fetch_sem.at[slot, a, 1 + part],
                    )
                )
        return copies

    def update(slot, n_columns, dst, i):
        @pl.loop(0, rows // 16)
        def _(t):
            r = pl.ds(pl.multiple_of(t * 16, 16), 16)
            piece = [fetched[slot, a, r, 0:n_columns] for a in range(4)]
            dst[i, r, :] = adam_update(*piece)

    def update_all(refs, kv_refs, n_columns, dst, after):
        @pl.loop(1, G + 1)
        def _(i):
            slot = lax.rem(i, 2)
            for copy in fetch(refs, kv_refs, i, slot):
                copy.wait()

            @pl.when(i < G)
            def _():
                for copy in fetch(refs, kv_refs, i + 1, 1 - slot):
                    copy.start()

            update(slot, n_columns, dst, i - 1)
            after(i)

    for copy in fetch((qp, qg, qm, qs), (kp, kg, km, ks), 1, 1):
        copy.start()

    squares = jnp.zeros((tokens, 1), jnp.float32)
    for c in range(S * NP):
        v = hidden[:, c * strip : (c + 1) * strip].astype(jnp.float32)
        squares += jnp.sum(v * v, axis=-1, keepdims=True)
    factor = lax.rsqrt(squares / (S * NP * strip) + norm_eps)
    for c in range(S * NP):
        at = slice(c * strip, (c + 1) * strip)
        v = hidden[:, at].astype(jnp.float32) * factor * norm_gain[0:1, at]
        x_send[c % NP, :, (c // NP) * strip : (c // NP + 1) * strip] = v.astype(jnp.bfloat16)

    pl.semaphore_wait(barrier, G - 1 + NP - 1)

    @pl.when(s == p)
    def _():
        for d in range(1, S):
            remote(
                length, length_here, l_ssem.at[d], l_rsem, (lax.rem(s + d, S), p, l)
            ).start()

    def x_copy(q, src_plane, d):
        return remote(
            x_send.at[q], normed.at[j, src_plane], x_ssem.at[d], x_rsem.at[src_plane], at_plane(q)
        )

    for d in range(1, NP):
        x_copy(lax.rem(p + d, NP), p, d).start()
    own_x = pltpu.make_async_copy(x_send.at[p], normed.at[j, p], local_sem.at[0])
    own_x.start()

    def w_copy(i):
        dest = lax.rem(j + i, G)
        return remote(
            w_send.at[i - 1], w_all.at[j], w_ssem.at[i - 1], w_rsem.at[j], member(dest)
        )

    def after_w(i):
        @pl.when(i < G)
        def _():
            w_copy(i).start()

    update_all((qp, qg, qm, qs), (kp, kg, km, ks), width, w_send, after_w)
    own_w = pltpu.make_async_copy(w_send.at[G - 1], w_all.at[j], local_sem.at[1])
    own_w.start()
    for copy in fetch((op, og, om, os_), (), 1, 1):
        copy.start()

    for d in range(1, NP):
        src_plane = lax.rem(p + d, NP)
        remote(
            x_send.at[src_plane],
            normed.at[j, src_plane],
            x_ssem.at[d],
            x_rsem.at[src_plane],
            at_plane(src_plane),
        ).wait_recv()
    own_x.wait()

    def g_copy(block, ssem, device):
        return remote(normed.at[block], normed.at[block], ssem, g_rsem.at[block], device)

    for n, (sec, lane) in enumerate(others):
        g_copy(j, g_ssem.at[n], (sec, p, lane)).start()
    g_copy(j, f_ssem.at[0], (sibling, p, l)).start()

    update_all((op, og, om, os_), (), hc, o_send, lambda i: None)

    for n, (sec, lane) in enumerate(others):
        block = sec * L + lane
        g_copy(block, g_ssem.at[n], (sec, p, lane)).wait_recv()
        g_copy(block, f_ssem.at[n + 1], (sibling, p, l)).start()
    for d in range(1, G):
        src = lax.rem(j + d, G)
        remote(w_send.at[0], w_all.at[src], w_ssem.at[0], w_rsem.at[src], member(src)).wait_recv()
    own_w.wait()
    for n, (sec, lane) in enumerate(same_core):
        block = (sec + 1 - 2 * core) * L + lane
        g_copy(block, f_ssem.at[n], (sibling, p, l)).wait_recv()

    def o_copy(i):
        dest = lax.rem(j + i, G)
        return remote(
            o_send.at[i - 1], o_all.at[j], o_ssem.at[i - 1], o_rsem.at[j], member(dest)
        )

    for i in range(1, G):
        o_copy(i).start()
    own_o = pltpu.make_async_copy(o_send.at[G - 1], o_all.at[j], local_sem.at[2])
    own_o.start()

    def product(prompt):
        x = normed[pl.ds(prompt * L, L)].reshape(seq, G * rows)
        w = w_all[...].reshape(G * rows, width)
        return jnp.dot(x, w, preferred_element_type=jnp.float32)

    def p_copy(d):
        q = lax.rem(p + d, NP)
        return remote(
            part_send.at[d - 1], part_recv.at[p], p_ssem.at[d - 1], p_rsem.at[p], at_plane(q)
        )

    @pl.loop(1, NP)
    def _(d):
        part_send[d - 1] = product(lax.rem(p + d, NP)).astype(jnp.bfloat16)
        p_copy(d).start()

    total[...] = product(p)
    for d in range(1, NP):
        q = lax.rem(p + d, NP)
        remote(
            part_send.at[0], part_recv.at[q], p_ssem.at[0], p_rsem.at[q], at_plane(q)
        ).wait_recv()
        total[...] += part_recv[q].astype(jnp.float32)

    @pl.when(s == p)
    def _():
        length_here[...] = length[...]
        for d in range(1, S):
            remote(
                length, length_here, l_ssem.at[d], l_rsem, (lax.rem(s + d, S), p, l)
            ).wait_send()

    @pl.when(s != p)
    def _():
        remote(length, length_here, l_ssem.at[0], l_rsem, (p, p, l)).wait_recv()

    def rotate(x):
        return (x * cosine[...] + pltpu.roll(x, HEAD_DIMENSION // 2, 1) * sine[...]).astype(
            jnp.bfloat16
        )

    key_rows = rotate(total[:, hc : hc + HEAD_DIMENSION])
    value_rows = total[:, hc + HEAD_DIMENSION :].astype(jnp.bfloat16)
    limit = jnp.concatenate([length_here[0:1, :]] * (seq // 128), axis=1)
    column = columns_at[0:1, :]
    allowed = (column <= rows_at[...]) & (column < limit)
    for h in range(hc // HEAD_DIMENSION):
        at = slice(h * HEAD_DIMENSION, (h + 1) * HEAD_DIMENSION)
        scores = lax.dot_general(
            rotate(total[:, at]),
            key_rows,
            (((1,), (1,)), ((), ())),
            preferred_element_type=jnp.float32,
        ) / math.sqrt(HEAD_DIMENSION)
        scores = jnp.where(allowed, scores, masked_score)
        exponent = jnp.exp(scores - jnp.max(scores, axis=-1, keepdims=True))
        attention = (exponent / jnp.sum(exponent, axis=-1, keepdims=True)).astype(jnp.bfloat16)
        heads[p, :, at] = jnp.dot(
            attention, value_rows, preferred_element_type=jnp.float32
        ).astype(jnp.bfloat16)

    for d in range(1, NP):
        remote(
            heads.at[p], heads.at[p], h_ssem.at[d], h_rsem.at[p], at_plane(lax.rem(p + d, NP))
        ).start()

    for d in range(1, G):
        src = lax.rem(j + d, G)
        remote(o_send.at[0], o_all.at[src], o_ssem.at[0], o_rsem.at[src], member(src)).wait_recv()
    own_o.wait()

    def heads_wait(q):
        @pl.when(q != p)
        def _():
            remote(heads.at[q], heads.at[q], h_ssem.at[0], h_rsem.at[q], at_plane(q)).wait_recv()

    def features(prompt, b):
        return lax.dot_general(
            heads[prompt], o_all[b], (((1,), (1,)), ((), ())), preferred_element_type=jnp.float32
        )

    def b_copy(e):
        return remote(
            pair_send.at[e], pair_recv.at[e], b_ssem.at[e], b_rsem.at[e], (sibling, p, l)
        )

    for e in range(half):
        prompt = 2 * lax.rem(pair + e, half) + 1 - core
        heads_wait(prompt)

        @pl.loop(0, G)
        def _(b):
            at = pl.ds(pl.multiple_of(b * rows, 128), rows)
            pair_send[e, :, at] = features(prompt, b).astype(jnp.bfloat16)

        b_copy(e).start()

    here = pair * L + l

    def r_copy(da, dl, n):
        sec, lane = same_core[da * L + dl]
        return remote(
            red_send.at[da, lane], red_recv.at[here], r_ssem.at[n], r_rsem.at[here], (sec, p, lane)
        )

    for e in list(range(1, half)) + [0]:
        prompt = 2 * lax.rem(pair + e, half) + core
        heads_wait(prompt)
        b_copy(e).wait_recv()

        @pl.loop(0, G)
        def _(b):
            at = pl.ds(pl.multiple_of(b * rows, 128), rows)
            value = features(prompt, b) + pair_recv[e, :, at].astype(jnp.float32)
            red_send[e, :, :, at] = value.astype(jnp.bfloat16).reshape(L, seq // L, rows)

        for dl in range(L):
            if e or dl:
                r_copy(e, dl, e * L + dl).start()

    summed = red_send[0, l].astype(jnp.float32)
    for n in range(1, half * L):
        sec, lane = same_core[n]
        src = (sec // 2) * L + lane
        remote(
            red_send.at[0, l], red_recv.at[src], r_ssem.at[0], r_rsem.at[src], (sec, p, lane)
        ).wait_recv()
        summed += red_recv[src].astype(jnp.float32)
    z_send[...] = summed.astype(jnp.bfloat16).reshape(NP, tokens, G * rows)

    def z_copy(q, d):
        return remote(z_send.at[q], z_recv.at[p], z_ssem.at[d], z_rsem.at[p], at_plane(q))

    for d in range(1, NP):
        z_copy(lax.rem(p + d, NP), d).start()
    z_recv[p] = z_send[p]
    for d in range(1, NP):
        q = lax.rem(p + d, NP)
        remote(z_send.at[q], z_recv.at[q], z_ssem.at[d], z_rsem.at[q], at_plane(q)).wait_recv()
    for c in range(S * NP):
        out[:, c * strip : (c + 1) * strip] = z_recv[
            c % NP, :, (c // NP) * strip : (c // NP + 1) * strip
        ]

    for d in range(1, NP):
        q = lax.rem(p + d, NP)
        x_copy(q, p, d).wait_send()
        p_copy(d).wait_send()
        remote(heads.at[p], heads.at[p], h_ssem.at[d], h_rsem.at[p], at_plane(q)).wait_send()
        z_copy(q, d).wait_send()
    for i in range(1, G):
        w_copy(i).wait_send()
        o_copy(i).wait_send()
    for n, (sec, lane) in enumerate(others):
        g_copy(j, g_ssem.at[n], (sec, p, lane)).wait_send()
    for n, (sec, lane) in enumerate(same_core):
        g_copy(sec * L + lane, f_ssem.at[n], (sibling, p, l)).wait_send()
    for e in range(half):
        b_copy(e).wait_send()
    for n in range(1, half * L):
        r_copy(n // L, n % L, n).wait_send()


def fused(hidden, norm_gain, lengths, *weights):
    S, NP, L = (lax.axis_size(a) for a in ("section", "plane", "lane"))
    G = S * L
    half = S // 2
    rows = weights[0].shape[0]
    hc = weights[0].shape[1] // G
    width = hc + 2 * HEAD_DIMENSION
    tokens = hidden.shape[1]
    seq = tokens * NP * L
    order = np.arange(seq).reshape(NP, L, tokens).transpose(1, 0, 2).reshape(seq)
    cosine, sine = rope_tables(order)
    rows_at = np.broadcast_to(order.astype(np.int32)[:, None], (seq, seq))
    columns_at = np.broadcast_to(order.astype(np.int32)[None, :], (8, seq))
    length = jnp.broadcast_to(lengths[:, None], (8, 128))
    bf, f32 = jnp.bfloat16, jnp.float32
    dma = pltpu.SemaphoreType.DMA
    vmem = pl.BlockSpec(memory_space=pltpu.VMEM)
    hbm = pl.BlockSpec(memory_space=pl.ANY)
    scratch = [
        pltpu.VMEM((2, 4, rows, width), f32),
        pltpu.VMEM((G, rows, width), bf),
        pltpu.VMEM((G, rows, width), bf),
        pltpu.VMEM((G, rows, hc), bf),
        pltpu.VMEM((G, rows, hc), bf),
        pltpu.VMEM((NP, tokens, G * rows), bf),
        pltpu.VMEM((G, NP, tokens, G * rows), bf),
        pltpu.VMEM((NP - 1, seq, width), bf),
        pltpu.VMEM((NP, seq, width), bf),
        pltpu.VMEM((seq, width), f32),
        pltpu.VMEM((NP, seq, hc), bf),
        pltpu.VMEM((half, seq, G * rows), bf),
        pltpu.VMEM((half, seq, G * rows), bf),
        pltpu.VMEM((half, L, seq // L, G * rows), bf),
        pltpu.VMEM((half * L, seq // L, G * rows), bf),
        pltpu.VMEM((NP, tokens, G * rows), bf),
        pltpu.VMEM((NP, tokens, G * rows), bf),
        pltpu.VMEM((8, 128), jnp.int32),
        dma((2, 4, 3)),
        dma((3,)),
        dma((G,)),
        dma((G,)),
        dma((G,)),
        dma((G,)),
        dma((NP,)),
        dma((NP,)),
        dma((half * L,)),
        dma((G,)),
        dma((half * L,)),
        dma((NP,)),
        dma((NP,)),
        dma((NP,)),
        dma((NP,)),
        dma((half,)),
        dma((half,)),
        dma((half * L,)),
        dma((half * L,)),
        dma((NP,)),
        dma((NP,)),
        dma((S,)),
        dma,
    ]
    result = pl.pallas_call(
        functools.partial(block_kernel, (S, NP, L)),
        out_shape=jax.ShapeDtypeStruct(hidden.shape[1:], bf),
        in_specs=[vmem] * 7 + [hbm] * 12,
        out_specs=vmem,
        scratch_shapes=scratch,
        compiler_params=pltpu.CompilerParams(
            collective_id=0, has_side_effects=True, vmem_limit_bytes=58 * 2**20
        ),
        cost_estimate=pl.CostEstimate(
            flops=8 * 10**9, bytes_accessed=4 * 10**7, transcendentals=10**6
        ),
    )(
        hidden[0],
        norm_gain[None, :],
        length,
        jnp.asarray(cosine),
        jnp.asarray(sine),
        jnp.asarray(rows_at),
        jnp.asarray(columns_at),
        *weights,
    )
    return result[None]


def layer(hidden, norm_gain, lengths, *weights):
    whole_tiles = (
        hidden.shape[1] % 16 == 0
        and weights[0].shape[0] % 128 == 0
        and lax.axis_size("section") % 2 == 0
    )
    return (fused if whole_tiles else on_device)(hidden, norm_gain, lengths, *weights)


def solution(mesh):
    sections, tensors = mesh.shape["section"], mesh.shape["tensor"]
    lanes = tensors // sections
    grid = Mesh(
        mesh.devices.reshape(sections, tensors // lanes, lanes), ("section", "plane", "lane")
    )
    row_spec = P(("section", "plane", "lane"), None)
    token_spec = P("section", ("plane", "lane"), None)
    return jax.shard_map(
        layer,
        mesh=grid,
        in_specs=(token_spec, P(), P("section")) + (row_spec,) * 12,
        out_specs=token_spec,
        check_vma=False,
    )
```

```python
import functools
import math

import jax
import jax.numpy as jnp
import numpy as np
from jax import lax
from jax.experimental import pallas as pl
from jax.experimental.pallas import tpu as pltpu
from jax.sharding import Mesh, PartitionSpec as P

QUERY_HEADS_LOCAL = 32
KEYVAL_HEADS = 4
HEAD_DIMENSION = 128


learn_rate = 0.015
beta_one = 0.5
beta_two = 0.9
adam_step = 1000.0
adam_eps = 1e-08
decay_rate = 0.1
norm_eps = 1e-06
rope_base = 1000000.0
masked_score = -1e30


def adam_update(current, gradient, moment, second):
    moment_new = beta_one * moment + (1.0 - beta_one) * gradient
    second_new = beta_two * second + (1.0 - beta_two) * gradient * gradient
    corrected = moment_new / (1.0 - beta_one**adam_step)
    denominator = jnp.sqrt(second_new / (1.0 - beta_two**adam_step)) + adam_eps
    return (current - learn_rate * (corrected / denominator + decay_rate * current)).astype(
        jnp.bfloat16
    )


def normalize(hidden, norm_gain):
    values = hidden.astype(jnp.float32)
    factor = lax.rsqrt(jnp.mean(values * values, axis=-1, keepdims=True) + norm_eps)
    return (values * factor * norm_gain).astype(jnp.bfloat16)


def rotary_embed(values, token_positions):
    half_width = values.shape[-1] // 2
    frequency = rope_base ** (-jnp.arange(half_width, dtype=jnp.float32) * 2.0 / values.shape[-1])
    angles = token_positions.astype(jnp.float32)[:, None] * frequency[None, :]
    cosine_table = jnp.concatenate([jnp.cos(angles), jnp.cos(angles)], axis=-1)
    sine_table = jnp.concatenate([jnp.sin(angles), jnp.sin(angles)], axis=-1)
    first_half = values[..., :half_width]
    second_half = values[..., half_width:]
    rotated = jnp.concatenate([-second_half, first_half], axis=-1)
    return values * cosine_table + rotated * sine_table


def on_device(
    hidden,
    norm_gain,
    lengths,
    query_param,
    query_grad,
    query_moment,
    query_second,
    keyval_param,
    keyval_gradient,
    keyval_first_moment,
    keyval_second_moment,
    output_param,
    output_grad,
    output_moment,
    output_second,
):
    sections = lax.axis_size("section")
    planes = lax.axis_size("plane")
    lanes = lax.axis_size("lane")
    members = sections * lanes
    group = ("section", "lane")
    rows = query_param.shape[0]
    head_columns = query_param.shape[1] // members
    heads_here = head_columns // HEAD_DIMENSION
    tokens_here, model_width = hidden.shape[1:]
    sequence = tokens_here * planes * lanes

    query_weight = adam_update(query_param, query_grad, query_moment, query_second)
    keyval_matrix = adam_update(
        keyval_param, keyval_gradient, keyval_first_moment, keyval_second_moment
    )
    output_weight = adam_update(output_param, output_grad, output_moment, output_second)

    spread_heads = jnp.repeat(
        keyval_matrix.reshape(rows, 2, KEYVAL_HEADS, HEAD_DIMENSION),
        members // KEYVAL_HEADS,
        axis=2,
    )
    spread_heads = spread_heads.transpose(2, 0, 1, 3).reshape(members, rows, 2 * HEAD_DIMENSION)
    query_pieces = query_weight.reshape(rows, members, head_columns).transpose(1, 0, 2)
    output_pieces = output_weight.reshape(rows, members, head_columns).transpose(1, 0, 2)
    query_rows = lax.all_to_all(query_pieces, group, 0, 0, tiled=True)
    keyval_rows = lax.all_to_all(spread_heads, group, 0, 0, tiled=True)
    output_rows = lax.all_to_all(output_pieces, group, 0, 0, tiled=True)
    query_rows = query_rows.reshape(members * rows, head_columns)
    keyval_rows = keyval_rows.reshape(members * rows, 2 * HEAD_DIMENSION)
    output_rows = output_rows.reshape(members * rows, head_columns)

    local_rows = normalize(hidden[0], norm_gain)
    features = local_rows.reshape(tokens_here, sections, planes, lanes * rows)
    features = features.transpose(2, 0, 1, 3).reshape(planes, tokens_here, members * rows)
    features = lax.all_to_all(features, "plane", 0, 0, tiled=True)
    normed = lax.all_gather(features, group, axis=0, tiled=True)
    normed = normed.reshape(sections * sequence, members * rows)

    partial = jnp.concatenate(
        [
            jnp.dot(normed, query_rows, preferred_element_type=jnp.float32).astype(jnp.bfloat16),
            jnp.dot(normed, keyval_rows, preferred_element_type=jnp.float32).astype(jnp.bfloat16),
        ],
        axis=1,
    ).reshape(sections, sequence, head_columns + 2 * HEAD_DIMENSION)
    partial = lax.all_to_all(partial, "plane", 0, 0, tiled=True)
    total = jnp.sum(partial.astype(jnp.float32), axis=0)

    order = jnp.arange(sequence).reshape(planes, lanes, tokens_here)
    token_positions = order.transpose(1, 0, 2).reshape(sequence)
    length = lax.dynamic_index_in_dim(
        lax.all_gather(lengths, "section", axis=0, tiled=True), lax.axis_index("plane"), 0, False
    )
    query_heads = rotary_embed(
        total[:, :head_columns].reshape(sequence, heads_here, HEAD_DIMENSION).transpose(1, 0, 2),
        token_positions,
    ).astype(jnp.bfloat16)
    key_head_rows = rotary_embed(
        total[:, head_columns : head_columns + HEAD_DIMENSION], token_positions
    ).astype(jnp.bfloat16)
    value_head_rows = total[:, head_columns + HEAD_DIMENSION :].astype(jnp.bfloat16)
    scores = jnp.einsum(
        "hqd,kd->hqk", query_heads, key_head_rows, preferred_element_type=jnp.float32
    ) / math.sqrt(HEAD_DIMENSION)
    allowed = (token_positions[None, :] <= token_positions[:, None]) & (
        token_positions[None, :] < length
    )
    scores = jnp.where(allowed[None], scores, masked_score)
    row_max = jnp.max(scores, axis=-1, keepdims=True)
    exponent = jnp.exp(scores - row_max)
    attention = (exponent / jnp.sum(exponent, axis=-1, keepdims=True)).astype(jnp.bfloat16)
    head_out = jnp.einsum(
        "hqk,kd->hqd", attention, value_head_rows, preferred_element_type=jnp.float32
    ).astype(jnp.bfloat16)
    head_out = head_out.transpose(1, 0, 2).reshape(sequence, head_columns)

    all_heads = lax.all_gather(head_out, "plane", axis=0, tiled=True)
    feature_part = lax.dot_general(
        all_heads, output_rows, (((1,), (1,)), ((), ())), preferred_element_type=jnp.float32
    ).astype(jnp.bfloat16)
    feature_part = feature_part.reshape(members, planes * tokens_here, members * rows)
    feature_part = lax.all_to_all(feature_part, group, 0, 0, tiled=True)
    summed = jnp.sum(feature_part.astype(jnp.float32), axis=0).astype(jnp.bfloat16)
    arrived = lax.all_to_all(
        summed.reshape(planes, tokens_here, members * rows), "plane", 0, 0, tiled=True
    )
    ordered = arrived.reshape(planes, tokens_here, sections, lanes * rows).transpose(1, 2, 0, 3)
    return ordered.reshape(1, tokens_here, model_width)


def rope_tables(positions):
    half_width = HEAD_DIMENSION // 2
    frequency = (
        rope_base ** (-np.arange(half_width, dtype=np.float64) * 2.0 / HEAD_DIMENSION)
    ).astype(np.float32)
    angles = positions.astype(np.float32)[:, None] * frequency[None, :]
    cosine, sine = np.cos(angles), np.sin(angles)
    return (
        np.concatenate([cosine, cosine], axis=-1).astype(np.float32),
        np.concatenate([-sine, sine], axis=-1).astype(np.float32),
    )


def block_kernel(
    sizes,
    hidden,
    norm_gain,
    lengths,
    cosine,
    sine,
    qp,
    qg,
    qm,
    qs,
    kp,
    kg,
    km,
    ks,
    op,
    og,
    om,
    os_,
    out,
    fetched,
    a_send,
    a_all,
    w_send,
    w_all,
    o_send,
    o_all,
    x_send,
    normed,
    pa_send,
    pa_recv,
    pb_send,
    pb_recv,
    total_a,
    total_b,
    keyval,
    heads_a,
    heads_b,
    pair_send,
    pair_recv,
    red_send,
    red_recv,
    z_send,
    z_recv,
    length,
    length_here,
    fetch_sem,
    local_sem,
    a_ssem,
    a_rsem,
    w_ssem,
    w_rsem,
    o_ssem,
    o_rsem,
    x_ssem,
    x_rsem,
    g_ssem,
    g_rsem,
    f_ssem,
    pa_ssem,
    pa_rsem,
    pb_ssem,
    pb_rsem,
    k_ssem,
    k_rsem,
    ha_ssem,
    ha_rsem,
    hb_ssem,
    hb_rsem,
    b_ssem,
    b_rsem,
    r_ssem,
    r_rsem,
    z_ssem,
    z_rsem,
    l_ssem,
    l_rsem,
):
    S, NP, L = sizes
    G = S * L
    half = S // 2
    s, p, l = lax.axis_index("section"), lax.axis_index("plane"), lax.axis_index("lane")
    j = s * L + l
    core = lax.rem(s, 2)
    pair = s // 2
    sibling = s + 1 - 2 * core
    rows = qp.shape[0]
    split = w_all.shape[2]
    first = a_all.shape[2] - HEAD_DIMENSION
    hc = first + split
    tokens = hidden.shape[0]
    strip = L * rows
    seq = NP * tokens * L

    def member(m):
        return (m // L, p, lax.rem(m, L))

    def at_plane(q):
        return (s, q, l)

    def remote(src, dst, ssem, rsem, device):
        return pltpu.make_async_remote_copy(
            src_ref=src,
            dst_ref=dst,
            send_sem=ssem,
            recv_sem=rsem,
            device_id=device,
            device_id_type=pl.DeviceIdType.MESH,
        )

    same_core = []
    for da in range(half):
        for dl in range(L):
            sec = 2 * lax.rem(pair + da, half) + core
            lane = lax.rem(l + dl, L)
            same_core.append((sec, lane))
    others = same_core[1:]

    length[...] = jnp.full(length.shape, lengths[0], jnp.int32)

    barrier = pltpu.get_barrier_semaphore()
    for d in range(1, G):
        pl.semaphore_signal(
            barrier, inc=1, device_id=member(lax.rem(j + d, G)), device_id_type=pl.DeviceIdType.MESH
        )
    for d in range(1, NP):
        pl.semaphore_signal(
            barrier,
            inc=1,
            device_id=at_plane(lax.rem(p + d, NP)),
            device_id_type=pl.DeviceIdType.MESH,
        )

    def fetch(refs, kv_refs, begin, n_columns, i, slot):
        dest = lax.rem(j + i, G)
        sec, lane = dest // L, lax.rem(dest, L)
        chip = (sec // 2) * L + lane
        block = chip * 2 + lax.rem(sec, 2)
        copies = []
        for a, ref in enumerate(refs):
            copies.append(
                pltpu.make_async_copy(
                    ref.at[:, pl.ds(pl.multiple_of(block * hc + begin, 128), n_columns)],
                    fetched.at[slot, a, :, pl.ds(0, n_columns)],
                    fetch_sem.at[slot, a, 0],
                )
            )
        for a, ref in enumerate(kv_refs):
            head = lax.rem(sec, 2) * KEYVAL_HEADS + chip
            copies.append(
                pltpu.make_async_copy(
                    ref.at[:, pl.ds(pl.multiple_of(head * HEAD_DIMENSION, 128), HEAD_DIMENSION)],
                    fetched.at[slot, a, :, pl.ds(n_columns, HEAD_DIMENSION)],
                    fetch_sem.at[slot, a, 1],
                )
            )
        return copies

    def update_all(job, following, n_columns, dst, after):
        @pl.loop(1, G + 1)
        def _(i):
            slot = lax.rem(i, 2)
            for copy in fetch(*job, i, slot):
                copy.wait()

            @pl.when(i < G)
            def _():
                for copy in fetch(*job, i + 1, 1 - slot):
                    copy.start()

            if following is not None:

                @pl.when(i == G)
                def _():
                    for copy in fetch(*following, 1, 1):
                        copy.start()

            @pl.loop(0, rows // 16)
            def _(t):
                r = pl.ds(pl.multiple_of(t * 16, 16), 16)
                piece = [fetched[slot, a, r, 0:n_columns] for a in range(4)]
                dst[i - 1, r, :] = adam_update(*piece)

            after(i)

    query_refs, keyval_refs = (qp, qg, qm, qs), (kp, kg, km, ks)
    job_a = (query_refs, keyval_refs, 0, first)
    job_w = (query_refs, (), first, split)
    job_o = ((op, og, om, os_), (), 0, hc)
    for copy in fetch(*job_a, 1, 1):
        copy.start()

    squares = jnp.zeros((tokens, 1), jnp.float32)
    for c in range(S * NP):
        v = hidden[:, c * strip : (c + 1) * strip].astype(jnp.float32)
        squares += jnp.sum(v * v, axis=-1, keepdims=True)
    factor = lax.rsqrt(squares / (S * NP * strip) + norm_eps)
    for c in range(S * NP):
        at = slice(c * strip, (c + 1) * strip)
        v = hidden[:, at].astype(jnp.float32) * factor * norm_gain[0:1, at]
        x_send[c % NP, :, (c // NP) * strip : (c // NP + 1) * strip] = v.astype(jnp.bfloat16)

    pl.semaphore_wait(barrier, G - 1 + NP - 1)

    @pl.when(s == p)
    def _():
        for d in range(1, S):
            remote(
                length, length_here, l_ssem.at[d], l_rsem, (lax.rem(s + d, S), p, l)
            ).start()

    def x_copy(q, src_plane, d):
        return remote(
            x_send.at[q], normed.at[j, src_plane], x_ssem.at[d], x_rsem.at[src_plane], at_plane(q)
        )

    for d in range(1, NP):
        x_copy(lax.rem(p + d, NP), p, d).start()
    own_x = pltpu.make_async_copy(x_send.at[p], normed.at[j, p], local_sem.at[0])
    own_x.start()

    def weight_copies(send, gathered, ssem, rsem):
        def copy(i):
            return remote(
                send.at[i - 1],
                gathered.at[j],
                ssem.at[i - 1],
                rsem.at[j],
                member(lax.rem(j + i, G)),
            )

        return copy

    def weight_wait(send, gathered, ssem, rsem):
        for d in range(1, G):
            src = lax.rem(j + d, G)
            remote(
                send.at[0], gathered.at[src], ssem.at[0], rsem.at[src], member(src)
            ).wait_recv()

    a_copy = weight_copies(a_send, a_all, a_ssem, a_rsem)
    w_copy = weight_copies(w_send, w_all, w_ssem, w_rsem)
    o_copy = weight_copies(o_send, o_all, o_ssem, o_rsem)

    def after_a(i):
        @pl.when(i < G)
        def _():
            a_copy(i).start()

    update_all(job_a, job_w, first + HEAD_DIMENSION, a_send, after_a)
    own_a = pltpu.make_async_copy(a_send.at[G - 1], a_all.at[j], local_sem.at[1])
    own_a.start()
    update_all(job_w, job_o, split, w_send, lambda i: None)
    own_w = pltpu.make_async_copy(w_send.at[G - 1], w_all.at[j], local_sem.at[2])
    own_w.start()

    for d in range(1, NP):
        src_plane = lax.rem(p + d, NP)
        remote(
            x_send.at[src_plane],
            normed.at[j, src_plane],
            x_ssem.at[d],
            x_rsem.at[src_plane],
            at_plane(src_plane),
        ).wait_recv()
    own_x.wait()

    def g_copy(block, ssem, device):
        return remote(normed.at[block], normed.at[block], ssem, g_rsem.at[block], device)

    for n, (sec, lane) in enumerate(others):
        g_copy(j, g_ssem.at[n], (sec, p, lane)).start()
    g_copy(j, f_ssem.at[0], (sibling, p, l)).start()

    update_all(job_o, None, hc, o_send, lambda i: None)
    own_o = pltpu.make_async_copy(o_send.at[G - 1], o_all.at[j], local_sem.at[3])
    own_o.start()

    for n, (sec, lane) in enumerate(others):
        block = sec * L + lane
        g_copy(block, g_ssem.at[n], (sec, p, lane)).wait_recv()
        g_copy(block, f_ssem.at[n + 1], (sibling, p, l)).start()
    for i in range(1, G):
        w_copy(i).start()
    weight_wait(a_send, a_all, a_ssem, a_rsem)
    own_a.wait()
    for n, (sec, lane) in enumerate(same_core):
        block = (sec + 1 - 2 * core) * L + lane
        g_copy(block, f_ssem.at[n], (sibling, p, l)).wait_recv()

    def product(prompt, weight):
        x = normed[pl.ds(prompt * L, L)].reshape(seq, G * rows)
        w = weight[...].reshape(G * rows, weight.shape[2])
        return jnp.dot(x, w, preferred_element_type=jnp.float32)

    def part_copy(send, recv, ssem, rsem, d):
        q = lax.rem(p + d, NP)
        return remote(send.at[d - 1], recv.at[p], ssem.at[d - 1], rsem.at[p], at_plane(q))

    def spread(weight, send, recv, ssem, rsem, own):
        @pl.loop(1, NP)
        def _(d):
            send[d - 1] = product(lax.rem(p + d, NP), weight).astype(jnp.bfloat16)
            part_copy(send, recv, ssem, rsem, d).start()

        own[...] = product(p, weight)

    def collect(send, recv, ssem, rsem, own):
        for d in range(1, NP):
            q = lax.rem(p + d, NP)
            remote(send.at[0], recv.at[q], ssem.at[0], rsem.at[q], at_plane(q)).wait_recv()
            own[...] += recv[q].astype(jnp.float32)

    spread(a_all, pa_send, pa_recv, pa_ssem, pa_rsem, total_a)
    weight_wait(w_send, w_all, w_ssem, w_rsem)
    own_w.wait()
    for i in range(1, G):
        o_copy(i).start()
    spread(w_all, pb_send, pb_recv, pb_ssem, pb_rsem, total_b)
    collect(pa_send, pa_recv, pa_ssem, pa_rsem, total_a)

    @pl.when(s == p)
    def _():
        length_here[...] = length[...]
        for d in range(1, S):
            remote(
                length, length_here, l_ssem.at[d], l_rsem, (lax.rem(s + d, S), p, l)
            ).wait_send()

    @pl.when(s != p)
    def _():
        remote(length, length_here, l_ssem.at[0], l_rsem, (p, p, l)).wait_recv()

    def rotate(x):
        return (x * cosine[...] + pltpu.roll(x, HEAD_DIMENSION // 2, 1) * sine[...]).astype(
            jnp.bfloat16
        )

    raw = total_a[:, first:]
    keyval[core] = jnp.where(core == 0, rotate(raw), raw.astype(jnp.bfloat16))

    def k_copy(index):
        return remote(keyval.at[index], keyval.at[index], k_ssem, k_rsem, (sibling, p, l))

    k_copy(core).start()

    def positions(index):
        place = index
        for block in range(1, L * NP):
            here, before = (
                ((b % NP) * L + b // NP) * tokens - b * tokens for b in (block, block - 1)
            )
            place += jnp.where(index >= block * tokens, here - before, 0)
        return place

    column = positions(lax.broadcasted_iota(jnp.int32, (1, seq), 1))
    row = positions(lax.broadcasted_iota(jnp.int32, (seq, 1), 0))
    limit = jnp.concatenate([length_here[0:1, :]] * (seq // 128), axis=1)
    allowed = (column <= row) & (column < limit)
    k_copy(1 - core).wait_recv()

    def attend(own, n_columns, gathered):
        for h in range(n_columns // HEAD_DIMENSION):
            at = slice(h * HEAD_DIMENSION, (h + 1) * HEAD_DIMENSION)
            scores = lax.dot_general(
                rotate(own[:, at]),
                keyval[0],
                (((1,), (1,)), ((), ())),
                preferred_element_type=jnp.float32,
            ) / math.sqrt(HEAD_DIMENSION)
            scores = jnp.where(allowed, scores, masked_score)
            exponent = jnp.exp(scores - jnp.max(scores, axis=-1, keepdims=True))
            attention = exponent / jnp.sum(exponent, axis=-1, keepdims=True)
            gathered[p, :, at] = jnp.dot(
                attention.astype(jnp.bfloat16), keyval[1], preferred_element_type=jnp.float32
            ).astype(jnp.bfloat16)

    def head_copy(gathered, ssem, rsem, d):
        return remote(
            gathered.at[p], gathered.at[p], ssem.at[d], rsem.at[p], at_plane(lax.rem(p + d, NP))
        )

    attend(total_a, first, heads_a)
    for d in range(1, NP):
        head_copy(heads_a, ha_ssem, ha_rsem, d).start()
    collect(pb_send, pb_recv, pb_ssem, pb_rsem, total_b)
    attend(total_b, split, heads_b)
    for d in range(1, NP):
        head_copy(heads_b, hb_ssem, hb_rsem, d).start()

    weight_wait(o_send, o_all, o_ssem, o_rsem)
    own_o.wait()

    def heads_wait(q):
        @pl.when(q != p)
        def _():
            for gathered, ssem, rsem in ((heads_a, ha_ssem, ha_rsem), (heads_b, hb_ssem, hb_rsem)):
                remote(
                    gathered.at[q], gathered.at[q], ssem.at[0], rsem.at[q], at_plane(q)
                ).wait_recv()

    def features(prompt, b):
        over = (((1,), (1,)), ((), ()))
        return lax.dot_general(
            heads_a[prompt], o_all[b, :, 0:first], over, preferred_element_type=jnp.float32
        ) + lax.dot_general(
            heads_b[prompt], o_all[b, :, first:], over, preferred_element_type=jnp.float32
        )

    def b_copy(e):
        return remote(
            pair_send.at[e], pair_recv.at[e], b_ssem.at[e], b_rsem.at[e], (sibling, p, l)
        )

    here = pair * L + l

    def r_copy(e, dl, start):
        chip = lax.rem(p // 2 + e, half)
        lane = lax.rem(l + dl, L)

        @pl.when((chip * L + lane) != here)
        def _():
            copy = remote(
                red_send.at[e, lane],
                red_recv.at[here],
                r_ssem.at[e, dl],
                r_rsem.at[here],
                (2 * chip + core, p, lane),
            )
            if start:
                copy.start()
            else:
                copy.wait_send()

    for e in range(half):
        theirs = 2 * lax.rem(p // 2 + e, half) + 1 - core
        mine = 2 * lax.rem(p // 2 + e, half) + core
        heads_wait(theirs)

        @pl.loop(0, G)
        def _(b):
            at = pl.ds(pl.multiple_of(b * rows, 128), rows)
            pair_send[e, :, at] = features(theirs, b).astype(jnp.bfloat16)

        b_copy(e).start()
        heads_wait(mine)
        b_copy(e).wait_recv()

        @pl.loop(0, G)
        def _(b):
            at = pl.ds(pl.multiple_of(b * rows, 128), rows)
            value = features(mine, b) + pair_recv[e, :, at].astype(jnp.float32)
            red_send[e, :, :, at] = value.astype(jnp.bfloat16).reshape(L, seq // L, rows)

        for dl in range(L):
            r_copy(e, dl, True)

    summed = red_send[lax.rem(pair + half - p // 2, half), l].astype(jnp.float32)
    for sec, lane in others:
        src = (sec // 2) * L + lane
        remote(
            red_send.at[0, l], red_recv.at[src], r_ssem.at[0, 0], r_rsem.at[src], (sec, p, lane)
        ).wait_recv()
        summed += red_recv[src].astype(jnp.float32)
    z_send[...] = summed.astype(jnp.bfloat16).reshape(NP, tokens, G * rows)

    def z_copy(q, d):
        return remote(z_send.at[q], z_recv.at[p], z_ssem.at[d], z_rsem.at[p], at_plane(q))

    for d in range(1, NP):
        z_copy(lax.rem(p + d, NP), d).start()
    z_recv[p] = z_send[p]
    for d in range(1, NP):
        q = lax.rem(p + d, NP)
        remote(z_send.at[q], z_recv.at[q], z_ssem.at[d], z_rsem.at[q], at_plane(q)).wait_recv()
    for c in range(S * NP):
        out[:, c * strip : (c + 1) * strip] = z_recv[
            c % NP, :, (c // NP) * strip : (c // NP + 1) * strip
        ]

    for d in range(1, NP):
        q = lax.rem(p + d, NP)
        x_copy(q, p, d).wait_send()
        part_copy(pa_send, pa_recv, pa_ssem, pa_rsem, d).wait_send()
        part_copy(pb_send, pb_recv, pb_ssem, pb_rsem, d).wait_send()
        head_copy(heads_a, ha_ssem, ha_rsem, d).wait_send()
        head_copy(heads_b, hb_ssem, hb_rsem, d).wait_send()
        z_copy(q, d).wait_send()
    for i in range(1, G):
        a_copy(i).wait_send()
        w_copy(i).wait_send()
        o_copy(i).wait_send()
    for n, (sec, lane) in enumerate(others):
        g_copy(j, g_ssem.at[n], (sec, p, lane)).wait_send()
    for n, (sec, lane) in enumerate(same_core):
        g_copy(sec * L + lane, f_ssem.at[n], (sibling, p, l)).wait_send()
    k_copy(core).wait_send()
    for e in range(half):
        b_copy(e).wait_send()
        for dl in range(L):
            r_copy(e, dl, False)


def fused(hidden, norm_gain, lengths, *weights):
    S, NP, L = (lax.axis_size(a) for a in ("section", "plane", "lane"))
    G = S * L
    half = S // 2
    rows = weights[0].shape[0]
    hc = weights[0].shape[1] // G
    first = hc // 2
    split = hc - first
    width = first + HEAD_DIMENSION
    tokens = hidden.shape[1]
    seq = tokens * NP * L
    order = np.arange(seq).reshape(NP, L, tokens).transpose(1, 0, 2).reshape(seq)
    cosine, sine = rope_tables(order)
    bf, f32 = jnp.bfloat16, jnp.float32
    dma = pltpu.SemaphoreType.DMA
    vmem = pl.BlockSpec(memory_space=pltpu.VMEM)
    hbm = pl.BlockSpec(memory_space=pl.ANY)
    smem = pl.BlockSpec(memory_space=pltpu.SMEM)
    scratch = [
        pltpu.VMEM((2, 4, rows, max(width, hc)), f32),
        pltpu.VMEM((G, rows, width), bf),
        pltpu.VMEM((G, rows, width), bf),
        pltpu.VMEM((G, rows, split), bf),
        pltpu.VMEM((G, rows, split), bf),
        pltpu.VMEM((G, rows, hc), bf),
        pltpu.VMEM((G, rows, hc), bf),
        pltpu.VMEM((NP, tokens, G * rows), bf),
        pltpu.VMEM((G, NP, tokens, G * rows), bf),
        pltpu.VMEM((NP - 1, seq, width), bf),
        pltpu.VMEM((NP, seq, width), bf),
        pltpu.VMEM((NP - 1, seq, split), bf),
        pltpu.VMEM((NP, seq, split), bf),
        pltpu.VMEM((seq, width), f32),
        pltpu.VMEM((seq, split), f32),
        pltpu.VMEM((2, seq, HEAD_DIMENSION), bf),
        pltpu.VMEM((NP, seq, first), bf),
        pltpu.VMEM((NP, seq, split), bf),
        pltpu.VMEM((half, seq, G * rows), bf),
        pltpu.VMEM((half, seq, G * rows), bf),
        pltpu.VMEM((half, L, seq // L, G * rows), bf),
        pltpu.VMEM((half * L, seq // L, G * rows), bf),
        pltpu.VMEM((NP, tokens, G * rows), bf),
        pltpu.VMEM((NP, tokens, G * rows), bf),
        pltpu.VMEM((8, 128), jnp.int32),
        pltpu.VMEM((8, 128), jnp.int32),
        dma((2, 4, 2)),
        dma((4,)),
    ]
    scratch += [dma((G,))] * 6
    scratch += [dma((NP,))] * 2
    scratch += [dma((half * L,)), dma((G,)), dma((half * L,))]
    scratch += [dma((NP,))] * 4
    scratch += [dma, dma]
    scratch += [dma((NP,))] * 4
    scratch += [dma((half,))] * 2
    scratch += [dma((half, L)), dma((half * L,))]
    scratch += [dma((NP,))] * 2
    scratch += [dma((S,)), dma]
    result = pl.pallas_call(
        functools.partial(block_kernel, (S, NP, L)),
        out_shape=jax.ShapeDtypeStruct(hidden.shape[1:], bf),
        in_specs=[vmem, vmem, smem, vmem, vmem] + [hbm] * 12,
        out_specs=vmem,
        scratch_shapes=scratch,
        compiler_params=pltpu.CompilerParams(
            collective_id=0, has_side_effects=True, vmem_limit_bytes=58 * 2**20
        ),
        cost_estimate=pl.CostEstimate(
            flops=8 * 10**9, bytes_accessed=4 * 10**7, transcendentals=10**6
        ),
    )(
        hidden[0],
        norm_gain[None, :],
        lengths,
        jnp.asarray(cosine),
        jnp.asarray(sine),
        *weights,
    )
    return result[None]


def layer(hidden, norm_gain, lengths, *weights):
    whole_tiles = (
        hidden.shape[1] % 16 == 0
        and weights[0].shape[0] % 128 == 0
        and lax.axis_size("section") % 2 == 0
        and lax.axis_size("section") * lax.axis_size("lane") == 2 * KEYVAL_HEADS
        and weights[0].shape[1] % (4 * HEAD_DIMENSION * KEYVAL_HEADS) == 0
    )
    return (fused if whole_tiles else on_device)(hidden, norm_gain, lengths, *weights)


def solution(mesh):
    sections, tensors = mesh.shape["section"], mesh.shape["tensor"]
    lanes = tensors // sections
    grid = Mesh(
        mesh.devices.reshape(sections, tensors // lanes, lanes), ("section", "plane", "lane")
    )
    row_spec = P(("section", "plane", "lane"), None)
    token_spec = P("section", ("plane", "lane"), None)
    return jax.shard_map(
        layer,
        mesh=grid,
        in_specs=(token_spec, P(), P("section")) + (row_spec,) * 12,
        out_specs=token_spec,
        check_vma=False,
    )
```

```python
import functools
import math

import jax
import jax.numpy as jnp
import numpy as np
from jax import lax
from jax.experimental import pallas as pl
from jax.experimental.pallas import tpu as pltpu
from jax.sharding import Mesh, PartitionSpec as P

QUERY_HEADS_LOCAL = 32
KEYVAL_HEADS = 4
HEAD_DIMENSION = 128


learn_rate = 0.015
beta_one = 0.5
beta_two = 0.9
adam_step = 1000.0
adam_eps = 1e-08
decay_rate = 0.1
norm_eps = 1e-06
rope_base = 1000000.0
masked_score = -1e30


def adam_update(current, gradient, moment, second):
    moment_new = beta_one * moment + (1.0 - beta_one) * gradient
    second_new = beta_two * second + (1.0 - beta_two) * gradient * gradient
    corrected = moment_new / (1.0 - beta_one**adam_step)
    denominator = jnp.sqrt(second_new / (1.0 - beta_two**adam_step)) + adam_eps
    return (current - learn_rate * (corrected / denominator + decay_rate * current)).astype(
        jnp.bfloat16
    )


def normalize(hidden, norm_gain):
    values = hidden.astype(jnp.float32)
    factor = lax.rsqrt(jnp.mean(values * values, axis=-1, keepdims=True) + norm_eps)
    return (values * factor * norm_gain).astype(jnp.bfloat16)


def rotary_embed(values, token_positions):
    half_width = values.shape[-1] // 2
    frequency = rope_base ** (-jnp.arange(half_width, dtype=jnp.float32) * 2.0 / values.shape[-1])
    angles = token_positions.astype(jnp.float32)[:, None] * frequency[None, :]
    cosine_table = jnp.concatenate([jnp.cos(angles), jnp.cos(angles)], axis=-1)
    sine_table = jnp.concatenate([jnp.sin(angles), jnp.sin(angles)], axis=-1)
    first_half = values[..., :half_width]
    second_half = values[..., half_width:]
    rotated = jnp.concatenate([-second_half, first_half], axis=-1)
    return values * cosine_table + rotated * sine_table


def on_device(
    hidden,
    norm_gain,
    lengths,
    query_param,
    query_grad,
    query_moment,
    query_second,
    keyval_param,
    keyval_gradient,
    keyval_first_moment,
    keyval_second_moment,
    output_param,
    output_grad,
    output_moment,
    output_second,
):
    sections = lax.axis_size("section")
    planes = lax.axis_size("plane")
    lanes = lax.axis_size("lane")
    members = sections * lanes
    group = ("section", "lane")
    rows = query_param.shape[0]
    head_columns = query_param.shape[1] // members
    heads_here = head_columns // HEAD_DIMENSION
    tokens_here, model_width = hidden.shape[1:]
    sequence = tokens_here * planes * lanes

    query_weight = adam_update(query_param, query_grad, query_moment, query_second)
    keyval_matrix = adam_update(
        keyval_param, keyval_gradient, keyval_first_moment, keyval_second_moment
    )
    output_weight = adam_update(output_param, output_grad, output_moment, output_second)

    spread_heads = jnp.repeat(
        keyval_matrix.reshape(rows, 2, KEYVAL_HEADS, HEAD_DIMENSION),
        members // KEYVAL_HEADS,
        axis=2,
    )
    spread_heads = spread_heads.transpose(2, 0, 1, 3).reshape(members, rows, 2 * HEAD_DIMENSION)
    query_pieces = query_weight.reshape(rows, members, head_columns).transpose(1, 0, 2)
    output_pieces = output_weight.reshape(rows, members, head_columns).transpose(1, 0, 2)
    query_rows = lax.all_to_all(query_pieces, group, 0, 0, tiled=True)
    keyval_rows = lax.all_to_all(spread_heads, group, 0, 0, tiled=True)
    output_rows = lax.all_to_all(output_pieces, group, 0, 0, tiled=True)
    query_rows = query_rows.reshape(members * rows, head_columns)
    keyval_rows = keyval_rows.reshape(members * rows, 2 * HEAD_DIMENSION)
    output_rows = output_rows.reshape(members * rows, head_columns)

    local_rows = normalize(hidden[0], norm_gain)
    features = local_rows.reshape(tokens_here, sections, planes, lanes * rows)
    features = features.transpose(2, 0, 1, 3).reshape(planes, tokens_here, members * rows)
    features = lax.all_to_all(features, "plane", 0, 0, tiled=True)
    normed = lax.all_gather(features, group, axis=0, tiled=True)
    normed = normed.reshape(sections * sequence, members * rows)

    partial = jnp.concatenate(
        [
            jnp.dot(normed, query_rows, preferred_element_type=jnp.float32).astype(jnp.bfloat16),
            jnp.dot(normed, keyval_rows, preferred_element_type=jnp.float32).astype(jnp.bfloat16),
        ],
        axis=1,
    ).reshape(sections, sequence, head_columns + 2 * HEAD_DIMENSION)
    partial = lax.all_to_all(partial, "plane", 0, 0, tiled=True)
    total = jnp.sum(partial.astype(jnp.float32), axis=0)

    order = jnp.arange(sequence).reshape(planes, lanes, tokens_here)
    token_positions = order.transpose(1, 0, 2).reshape(sequence)
    length = lax.dynamic_index_in_dim(
        lax.all_gather(lengths, "section", axis=0, tiled=True), lax.axis_index("plane"), 0, False
    )
    query_heads = rotary_embed(
        total[:, :head_columns].reshape(sequence, heads_here, HEAD_DIMENSION).transpose(1, 0, 2),
        token_positions,
    ).astype(jnp.bfloat16)
    key_head_rows = rotary_embed(
        total[:, head_columns : head_columns + HEAD_DIMENSION], token_positions
    ).astype(jnp.bfloat16)
    value_head_rows = total[:, head_columns + HEAD_DIMENSION :].astype(jnp.bfloat16)
    scores = jnp.einsum(
        "hqd,kd->hqk", query_heads, key_head_rows, preferred_element_type=jnp.float32
    ) / math.sqrt(HEAD_DIMENSION)
    allowed = (token_positions[None, :] <= token_positions[:, None]) & (
        token_positions[None, :] < length
    )
    scores = jnp.where(allowed[None], scores, masked_score)
    row_max = jnp.max(scores, axis=-1, keepdims=True)
    exponent = jnp.exp(scores - row_max)
    attention = (exponent / jnp.sum(exponent, axis=-1, keepdims=True)).astype(jnp.bfloat16)
    head_out = jnp.einsum(
        "hqk,kd->hqd", attention, value_head_rows, preferred_element_type=jnp.float32
    ).astype(jnp.bfloat16)
    head_out = head_out.transpose(1, 0, 2).reshape(sequence, head_columns)

    all_heads = lax.all_gather(head_out, "plane", axis=0, tiled=True)
    feature_part = lax.dot_general(
        all_heads, output_rows, (((1,), (1,)), ((), ())), preferred_element_type=jnp.float32
    ).astype(jnp.bfloat16)
    feature_part = feature_part.reshape(members, planes * tokens_here, members * rows)
    feature_part = lax.all_to_all(feature_part, group, 0, 0, tiled=True)
    summed = jnp.sum(feature_part.astype(jnp.float32), axis=0).astype(jnp.bfloat16)
    arrived = lax.all_to_all(
        summed.reshape(planes, tokens_here, members * rows), "plane", 0, 0, tiled=True
    )
    ordered = arrived.reshape(planes, tokens_here, sections, lanes * rows).transpose(1, 2, 0, 3)
    return ordered.reshape(1, tokens_here, model_width)


def rope_tables(positions):
    half_width = HEAD_DIMENSION // 2
    frequency = (
        rope_base ** (-np.arange(half_width, dtype=np.float64) * 2.0 / HEAD_DIMENSION)
    ).astype(np.float32)
    angles = positions.astype(np.float32)[:, None] * frequency[None, :]
    cosine, sine = np.cos(angles), np.sin(angles)
    return (
        np.concatenate([cosine, cosine], axis=-1).astype(np.float32),
        np.concatenate([-sine, sine], axis=-1).astype(np.float32),
    )


def block_kernel(
    sizes,
    hidden,
    norm_gain,
    lengths,
    cosine,
    sine,
    qp,
    qg,
    qm,
    qs,
    kp,
    kg,
    km,
    ks,
    op,
    og,
    om,
    os_,
    out,
    fetched,
    a_send,
    a_all,
    w_send,
    w_all,
    o_send,
    o_all,
    x_send,
    normed,
    pa_send,
    pa_recv,
    pb_send,
    pb_recv,
    total_a,
    total_b,
    keyval,
    heads_a,
    heads_b,
    pair_send,
    pair_recv,
    red_send,
    red_recv,
    z_send,
    z_recv,
    length,
    length_here,
    fetch_sem,
    local_sem,
    a_ssem,
    a_rsem,
    w_ssem,
    w_rsem,
    o_ssem,
    o_rsem,
    x_ssem,
    x_rsem,
    g_ssem,
    g_rsem,
    f_ssem,
    pa_ssem,
    pa_rsem,
    pb_ssem,
    pb_rsem,
    k_ssem,
    k_rsem,
    ha_ssem,
    ha_rsem,
    hb_ssem,
    hb_rsem,
    b_ssem,
    b_rsem,
    r_ssem,
    r_rsem,
    z_ssem,
    z_rsem,
    l_ssem,
    l_rsem,
):
    S, NP, L = sizes
    G = S * L
    half = S // 2
    s, p, l = lax.axis_index("section"), lax.axis_index("plane"), lax.axis_index("lane")
    j = s * L + l
    core = lax.rem(s, 2)
    pair = s // 2
    sibling = s + 1 - 2 * core
    rows = qp.shape[0]
    split = w_all.shape[2]
    first = a_all.shape[2] - HEAD_DIMENSION
    hc = first + split
    tokens = hidden.shape[0]
    strip = L * rows
    seq = NP * tokens * L

    def member(m):
        return (m // L, p, lax.rem(m, L))

    def at_plane(q):
        return (s, q, l)

    def remote(src, dst, ssem, rsem, device):
        return pltpu.make_async_remote_copy(
            src_ref=src,
            dst_ref=dst,
            send_sem=ssem,
            recv_sem=rsem,
            device_id=device,
            device_id_type=pl.DeviceIdType.MESH,
        )

    def section_of(plane):
        core_of = lax.rem(plane, 2)
        return 2 * lax.rem(plane // 2 + core_of, half) + core_of

    kept = section_of(p)

    same_core = []
    for da in range(half):
        for dl in range(L):
            sec = 2 * lax.rem(pair + da, half) + core
            lane = lax.rem(l + dl, L)
            same_core.append((sec, lane))
    others = same_core[1:]

    length[...] = jnp.full(length.shape, lengths[0], jnp.int32)

    barrier = pltpu.get_barrier_semaphore()
    for d in range(1, G):
        pl.semaphore_signal(
            barrier, inc=1, device_id=member(lax.rem(j + d, G)), device_id_type=pl.DeviceIdType.MESH
        )
    for d in range(1, NP):
        pl.semaphore_signal(
            barrier,
            inc=1,
            device_id=at_plane(lax.rem(p + d, NP)),
            device_id_type=pl.DeviceIdType.MESH,
        )

    def fetch(refs, kv_refs, begin, n_columns, i, slot):
        dest = lax.rem(j + i, G)
        sec, lane = dest // L, lax.rem(dest, L)
        chip = (sec // 2) * L + lane
        block = chip * 2 + lax.rem(sec, 2)
        copies = []
        for a, ref in enumerate(refs):
            copies.append(
                pltpu.make_async_copy(
                    ref.at[:, pl.ds(pl.multiple_of(block * hc + begin, 128), n_columns)],
                    fetched.at[slot, a, :, pl.ds(0, n_columns)],
                    fetch_sem.at[slot, a, 0],
                )
            )
        for a, ref in enumerate(kv_refs):
            head = lax.rem(sec, 2) * KEYVAL_HEADS + chip
            copies.append(
                pltpu.make_async_copy(
                    ref.at[:, pl.ds(pl.multiple_of(head * HEAD_DIMENSION, 128), HEAD_DIMENSION)],
                    fetched.at[slot, a, :, pl.ds(n_columns, HEAD_DIMENSION)],
                    fetch_sem.at[slot, a, 1],
                )
            )
        return copies

    def update_all(job, following, n_columns, dst, after):
        @pl.loop(1, G + 1)
        def _(i):
            slot = lax.rem(i, 2)
            for copy in fetch(*job, i, slot):
                copy.wait()

            @pl.when(i < G)
            def _():
                for copy in fetch(*job, i + 1, 1 - slot):
                    copy.start()

            if following is not None:

                @pl.when(i == G)
                def _():
                    for copy in fetch(*following, 1, 1):
                        copy.start()

            @pl.loop(0, rows // 16)
            def _(t):
                r = pl.ds(pl.multiple_of(t * 16, 16), 16)
                piece = [fetched[slot, a, r, 0:n_columns] for a in range(4)]
                dst[i - 1, r, :] = adam_update(*piece)

            after(i)

    query_refs, keyval_refs = (qp, qg, qm, qs), (kp, kg, km, ks)
    job_a = (query_refs, keyval_refs, 0, first)
    job_w = (query_refs, (), first, split)
    job_o = ((op, og, om, os_), (), 0, hc)
    for copy in fetch(*job_a, 1, 1):
        copy.start()

    squares = jnp.zeros((tokens, 1), jnp.float32)
    for c in range(S * NP):
        v = hidden[:, c * strip : (c + 1) * strip].astype(jnp.float32)
        squares += jnp.sum(v * v, axis=-1, keepdims=True)
    factor = lax.rsqrt(squares / (S * NP * strip) + norm_eps)
    for c in range(S * NP):
        at = slice(c * strip, (c + 1) * strip)
        v = hidden[:, at].astype(jnp.float32) * factor * norm_gain[0:1, at]
        x_send[c % NP, :, (c // NP) * strip : (c // NP + 1) * strip] = v.astype(jnp.bfloat16)

    pl.semaphore_wait(barrier, G - 1 + NP - 1)

    @pl.when(s == kept)
    def _():
        for d in range(1, S):
            remote(
                length, length_here, l_ssem.at[d], l_rsem, (lax.rem(s + d, S), p, l)
            ).start()

    def x_copy(q, src_plane, d):
        return remote(
            x_send.at[q], normed.at[j, src_plane], x_ssem.at[d], x_rsem.at[src_plane], at_plane(q)
        )

    for d in range(1, NP):
        x_copy(lax.rem(p + d, NP), p, d).start()
    own_x = pltpu.make_async_copy(x_send.at[p], normed.at[j, p], local_sem.at[0])
    own_x.start()

    def weight_copies(send, gathered, ssem, rsem):
        def copy(i):
            return remote(
                send.at[i - 1],
                gathered.at[j],
                ssem.at[i - 1],
                rsem.at[j],
                member(lax.rem(j + i, G)),
            )

        return copy

    def weight_wait(send, gathered, ssem, rsem):
        for d in range(1, G):
            src = lax.rem(j + d, G)
            remote(
                send.at[0], gathered.at[src], ssem.at[0], rsem.at[src], member(src)
            ).wait_recv()

    a_copy = weight_copies(a_send, a_all, a_ssem, a_rsem)
    w_copy = weight_copies(w_send, w_all, w_ssem, w_rsem)
    o_copy = weight_copies(o_send, o_all, o_ssem, o_rsem)

    def after_a(i):
        @pl.when(i < G)
        def _():
            a_copy(i).start()

    update_all(job_a, job_w, first + HEAD_DIMENSION, a_send, after_a)
    own_a = pltpu.make_async_copy(a_send.at[G - 1], a_all.at[j], local_sem.at[1])
    own_a.start()
    update_all(job_w, job_o, split, w_send, lambda i: None)
    own_w = pltpu.make_async_copy(w_send.at[G - 1], w_all.at[j], local_sem.at[2])
    own_w.start()

    for d in range(1, NP):
        src_plane = lax.rem(p + d, NP)
        remote(
            x_send.at[src_plane],
            normed.at[j, src_plane],
            x_ssem.at[d],
            x_rsem.at[src_plane],
            at_plane(src_plane),
        ).wait_recv()
    own_x.wait()

    def g_copy(block, ssem, device):
        return remote(normed.at[block], normed.at[block], ssem, g_rsem.at[block], device)

    for n, (sec, lane) in enumerate(others):
        g_copy(j, g_ssem.at[n], (sec, p, lane)).start()
    g_copy(j, f_ssem.at[0], (sibling, p, l)).start()

    update_all(job_o, None, hc, o_send, lambda i: None)
    own_o = pltpu.make_async_copy(o_send.at[G - 1], o_all.at[j], local_sem.at[3])
    own_o.start()

    for n, (sec, lane) in enumerate(others):
        block = sec * L + lane
        g_copy(block, g_ssem.at[n], (sec, p, lane)).wait_recv()
        g_copy(block, f_ssem.at[n + 1], (sibling, p, l)).start()
    for i in range(1, G):
        w_copy(i).start()
    weight_wait(a_send, a_all, a_ssem, a_rsem)
    own_a.wait()
    for n, (sec, lane) in enumerate(same_core):
        block = (sec + 1 - 2 * core) * L + lane
        g_copy(block, f_ssem.at[n], (sibling, p, l)).wait_recv()

    def product(plane, weight):
        x = normed[pl.ds(section_of(plane) * L, L)].reshape(seq, G * rows)
        w = weight[...].reshape(G * rows, weight.shape[2])
        return jnp.dot(x, w, preferred_element_type=jnp.float32)

    def part_copy(send, recv, ssem, rsem, d):
        q = lax.rem(p + d, NP)
        return remote(send.at[d - 1], recv.at[p], ssem.at[d - 1], rsem.at[p], at_plane(q))

    def spread(weight, send, recv, ssem, rsem, own):
        @pl.loop(1, NP)
        def _(d):
            send[d - 1] = product(lax.rem(p + d, NP), weight).astype(jnp.bfloat16)
            part_copy(send, recv, ssem, rsem, d).start()

        own[...] = product(p, weight)

    def collect(send, recv, ssem, rsem, own):
        for d in range(1, NP):
            q = lax.rem(p + d, NP)
            remote(send.at[0], recv.at[q], ssem.at[0], rsem.at[q], at_plane(q)).wait_recv()
            own[...] += recv[q].astype(jnp.float32)

    spread(a_all, pa_send, pa_recv, pa_ssem, pa_rsem, total_a)
    weight_wait(w_send, w_all, w_ssem, w_rsem)
    own_w.wait()
    for i in range(1, G):
        o_copy(i).start()
    spread(w_all, pb_send, pb_recv, pb_ssem, pb_rsem, total_b)
    collect(pa_send, pa_recv, pa_ssem, pa_rsem, total_a)

    @pl.when(s == kept)
    def _():
        length_here[...] = length[...]
        for d in range(1, S):
            remote(
                length, length_here, l_ssem.at[d], l_rsem, (lax.rem(s + d, S), p, l)
            ).wait_send()

    @pl.when(s != kept)
    def _():
        remote(length, length_here, l_ssem.at[0], l_rsem, (kept, p, l)).wait_recv()

    def rotate(x):
        return (x * cosine[...] + pltpu.roll(x, HEAD_DIMENSION // 2, 1) * sine[...]).astype(
            jnp.bfloat16
        )

    raw = total_a[:, first:]
    keyval[core] = jnp.where(core == 0, rotate(raw), raw.astype(jnp.bfloat16))

    def k_copy(index):
        return remote(keyval.at[index], keyval.at[index], k_ssem, k_rsem, (sibling, p, l))

    k_copy(core).start()

    def positions(index):
        place = index
        for block in range(1, L * NP):
            here, before = (
                ((b % NP) * L + b // NP) * tokens - b * tokens for b in (block, block - 1)
            )
            place += jnp.where(index >= block * tokens, here - before, 0)
        return place

    column = positions(lax.broadcasted_iota(jnp.int32, (1, seq), 1))
    row = positions(lax.broadcasted_iota(jnp.int32, (seq, 1), 0))
    limit = jnp.concatenate([length_here[0:1, :]] * (seq // 128), axis=1)
    allowed = (column <= row) & (column < limit)
    k_copy(1 - core).wait_recv()

    def attend(own, n_columns, gathered):
        for h in range(n_columns // HEAD_DIMENSION):
            at = slice(h * HEAD_DIMENSION, (h + 1) * HEAD_DIMENSION)
            scores = lax.dot_general(
                rotate(own[:, at]),
                keyval[0],
                (((1,), (1,)), ((), ())),
                preferred_element_type=jnp.float32,
            ) / math.sqrt(HEAD_DIMENSION)
            scores = jnp.where(allowed, scores, masked_score)
            exponent = jnp.exp(scores - jnp.max(scores, axis=-1, keepdims=True))
            attention = exponent / jnp.sum(exponent, axis=-1, keepdims=True)
            gathered[p, :, at] = jnp.dot(
                attention.astype(jnp.bfloat16), keyval[1], preferred_element_type=jnp.float32
            ).astype(jnp.bfloat16)

    def head_copy(gathered, ssem, rsem, d):
        return remote(
            gathered.at[p], gathered.at[p], ssem.at[d], rsem.at[p], at_plane(lax.rem(p + d, NP))
        )

    attend(total_a, first, heads_a)
    for d in range(1, NP):
        head_copy(heads_a, ha_ssem, ha_rsem, d).start()
    collect(pb_send, pb_recv, pb_ssem, pb_rsem, total_b)
    attend(total_b, split, heads_b)
    for d in range(1, NP):
        head_copy(heads_b, hb_ssem, hb_rsem, d).start()

    weight_wait(o_send, o_all, o_ssem, o_rsem)
    own_o.wait()

    def heads_wait(q):
        @pl.when(q != p)
        def _():
            for gathered, ssem, rsem in ((heads_a, ha_ssem, ha_rsem), (heads_b, hb_ssem, hb_rsem)):
                remote(
                    gathered.at[q], gathered.at[q], ssem.at[0], rsem.at[q], at_plane(q)
                ).wait_recv()

    def features(prompt, b):
        over = (((1,), (1,)), ((), ()))
        return lax.dot_general(
            heads_a[prompt], o_all[b, :, 0:first], over, preferred_element_type=jnp.float32
        ) + lax.dot_general(
            heads_b[prompt], o_all[b, :, first:], over, preferred_element_type=jnp.float32
        )

    def b_copy(e):
        return remote(
            pair_send.at[e], pair_recv.at[e], b_ssem.at[e], b_rsem.at[e], (sibling, p, l)
        )

    here = pair * L + l

    def r_copy(e, dl, start):
        chip = lax.rem(p // 2 + e + core, half)
        lane = lax.rem(l + dl, L)

        @pl.when((chip * L + lane) != here)
        def _():
            copy = remote(
                red_send.at[e, lane],
                red_recv.at[here],
                r_ssem.at[e, dl],
                r_rsem.at[here],
                (2 * chip + core, p, lane),
            )
            if start:
                copy.start()
            else:
                copy.wait_send()

    for e in range(half):
        theirs = 2 * lax.rem(p // 2 + e, half) + 1 - core
        mine = 2 * lax.rem(p // 2 + e, half) + core
        heads_wait(theirs)

        @pl.loop(0, G)
        def _(b):
            at = pl.ds(pl.multiple_of(b * rows, 128), rows)
            pair_send[e, :, at] = features(theirs, b).astype(jnp.bfloat16)

        b_copy(e).start()
        heads_wait(mine)
        b_copy(e).wait_recv()

        @pl.loop(0, G)
        def _(b):
            at = pl.ds(pl.multiple_of(b * rows, 128), rows)
            value = features(mine, b) + pair_recv[e, :, at].astype(jnp.float32)
            red_send[e, :, :, at] = value.astype(jnp.bfloat16).reshape(L, seq // L, rows)

        for dl in range(L):
            r_copy(e, dl, True)

    summed = red_send[lax.rem(pair + 2 * half - core - p // 2, half), l].astype(jnp.float32)
    for sec, lane in others:
        src = (sec // 2) * L + lane
        remote(
            red_send.at[0, l], red_recv.at[src], r_ssem.at[0, 0], r_rsem.at[src], (sec, p, lane)
        ).wait_recv()
        summed += red_recv[src].astype(jnp.float32)
    z_send[...] = summed.astype(jnp.bfloat16).reshape(NP, tokens, G * rows)

    def z_copy(q, d):
        return remote(z_send.at[q], z_recv.at[p], z_ssem.at[d], z_rsem.at[p], at_plane(q))

    for d in range(1, NP):
        z_copy(lax.rem(p + d, NP), d).start()
    z_recv[p] = z_send[p]
    for d in range(1, NP):
        q = lax.rem(p + d, NP)
        remote(z_send.at[q], z_recv.at[q], z_ssem.at[d], z_rsem.at[q], at_plane(q)).wait_recv()
    for c in range(S * NP):
        out[:, c * strip : (c + 1) * strip] = z_recv[
            c % NP, :, (c // NP) * strip : (c // NP + 1) * strip
        ]

    for d in range(1, NP):
        q = lax.rem(p + d, NP)
        x_copy(q, p, d).wait_send()
        part_copy(pa_send, pa_recv, pa_ssem, pa_rsem, d).wait_send()
        part_copy(pb_send, pb_recv, pb_ssem, pb_rsem, d).wait_send()
        head_copy(heads_a, ha_ssem, ha_rsem, d).wait_send()
        head_copy(heads_b, hb_ssem, hb_rsem, d).wait_send()
        z_copy(q, d).wait_send()
    for i in range(1, G):
        a_copy(i).wait_send()
        w_copy(i).wait_send()
        o_copy(i).wait_send()
    for n, (sec, lane) in enumerate(others):
        g_copy(j, g_ssem.at[n], (sec, p, lane)).wait_send()
    for n, (sec, lane) in enumerate(same_core):
        g_copy(sec * L + lane, f_ssem.at[n], (sibling, p, l)).wait_send()
    k_copy(core).wait_send()
    for e in range(half):
        b_copy(e).wait_send()
        for dl in range(L):
            r_copy(e, dl, False)


def fused(hidden, norm_gain, lengths, *weights):
    S, NP, L = (lax.axis_size(a) for a in ("section", "plane", "lane"))
    G = S * L
    half = S // 2
    rows = weights[0].shape[0]
    hc = weights[0].shape[1] // G
    first = hc // 2
    split = hc - first
    width = first + HEAD_DIMENSION
    tokens = hidden.shape[1]
    seq = tokens * NP * L
    order = np.arange(seq).reshape(NP, L, tokens).transpose(1, 0, 2).reshape(seq)
    cosine, sine = rope_tables(order)
    bf, f32 = jnp.bfloat16, jnp.float32
    dma = pltpu.SemaphoreType.DMA
    vmem = pl.BlockSpec(memory_space=pltpu.VMEM)
    hbm = pl.BlockSpec(memory_space=pl.ANY)
    smem = pl.BlockSpec(memory_space=pltpu.SMEM)
    scratch = [
        pltpu.VMEM((2, 4, rows, max(width, hc)), f32),
        pltpu.VMEM((G, rows, width), bf),
        pltpu.VMEM((G, rows, width), bf),
        pltpu.VMEM((G, rows, split), bf),
        pltpu.VMEM((G, rows, split), bf),
        pltpu.VMEM((G, rows, hc), bf),
        pltpu.VMEM((G, rows, hc), bf),
        pltpu.VMEM((NP, tokens, G * rows), bf),
        pltpu.VMEM((G, NP, tokens, G * rows), bf),
        pltpu.VMEM((NP - 1, seq, width), bf),
        pltpu.VMEM((NP, seq, width), bf),
        pltpu.VMEM((NP - 1, seq, split), bf),
        pltpu.VMEM((NP, seq, split), bf),
        pltpu.VMEM((seq, width), f32),
        pltpu.VMEM((seq, split), f32),
        pltpu.VMEM((2, seq, HEAD_DIMENSION), bf),
        pltpu.VMEM((NP, seq, first), bf),
        pltpu.VMEM((NP, seq, split), bf),
        pltpu.VMEM((half, seq, G * rows), bf),
        pltpu.VMEM((half, seq, G * rows), bf),
        pltpu.VMEM((half, L, seq // L, G * rows), bf),
        pltpu.VMEM((half * L, seq // L, G * rows), bf),
        pltpu.VMEM((NP, tokens, G * rows), bf),
        pltpu.VMEM((NP, tokens, G * rows), bf),
        pltpu.VMEM((8, 128), jnp.int32),
        pltpu.VMEM((8, 128), jnp.int32),
        dma((2, 4, 2)),
        dma((4,)),
    ]
    scratch += [dma((G,))] * 6
    scratch += [dma((NP,))] * 2
    scratch += [dma((half * L,)), dma((G,)), dma((half * L,))]
    scratch += [dma((NP,))] * 4
    scratch += [dma, dma]
    scratch += [dma((NP,))] * 4
    scratch += [dma((half,))] * 2
    scratch += [dma((half, L)), dma((half * L,))]
    scratch += [dma((NP,))] * 2
    scratch += [dma((S,)), dma]
    result = pl.pallas_call(
        functools.partial(block_kernel, (S, NP, L)),
        out_shape=jax.ShapeDtypeStruct(hidden.shape[1:], bf),
        in_specs=[vmem, vmem, smem, vmem, vmem] + [hbm] * 12,
        out_specs=vmem,
        scratch_shapes=scratch,
        compiler_params=pltpu.CompilerParams(
            collective_id=0, has_side_effects=True, vmem_limit_bytes=58 * 2**20
        ),
        cost_estimate=pl.CostEstimate(
            flops=8 * 10**9, bytes_accessed=4 * 10**7, transcendentals=10**6
        ),
    )(
        hidden[0],
        norm_gain[None, :],
        lengths,
        jnp.asarray(cosine),
        jnp.asarray(sine),
        *weights,
    )
    return result[None]


def layer(hidden, norm_gain, lengths, *weights):
    whole_tiles = (
        hidden.shape[1] % 16 == 0
        and weights[0].shape[0] % 128 == 0
        and lax.axis_size("section") % 2 == 0
        and lax.axis_size("section") * lax.axis_size("lane") == 2 * KEYVAL_HEADS
        and weights[0].shape[1] % (4 * HEAD_DIMENSION * KEYVAL_HEADS) == 0
    )
    return (fused if whole_tiles else on_device)(hidden, norm_gain, lengths, *weights)


def solution(mesh):
    sections, tensors = mesh.shape["section"], mesh.shape["tensor"]
    lanes = tensors // sections
    grid = Mesh(
        mesh.devices.reshape(sections, tensors // lanes, lanes), ("section", "plane", "lane")
    )
    row_spec = P(("section", "plane", "lane"), None)
    token_spec = P("section", ("plane", "lane"), None)
    return jax.shard_map(
        layer,
        mesh=grid,
        in_specs=(token_spec, P(), P("section")) + (row_spec,) * 12,
        out_specs=token_spec,
        check_vma=False,
    )
```

```python
import functools
import math

import jax
import jax.numpy as jnp
import numpy as np
from jax import lax
from jax.experimental import pallas as pl
from jax.experimental.pallas import tpu as pltpu
from jax.sharding import Mesh, PartitionSpec as P

QUERY_HEADS_LOCAL = 32
KEYVAL_HEADS = 4
HEAD_DIMENSION = 128


learn_rate = 0.015
beta_one = 0.5
beta_two = 0.9
adam_step = 1000.0
adam_eps = 1e-08
decay_rate = 0.1
norm_eps = 1e-06
rope_base = 1000000.0
masked_score = -1e30


def adam_update(current, gradient, moment, second):
    moment_new = beta_one * moment + (1.0 - beta_one) * gradient
    second_new = beta_two * second + (1.0 - beta_two) * gradient * gradient
    corrected = moment_new / (1.0 - beta_one**adam_step)
    denominator = jnp.sqrt(second_new / (1.0 - beta_two**adam_step)) + adam_eps
    return (current - learn_rate * (corrected / denominator + decay_rate * current)).astype(
        jnp.bfloat16
    )


def normalize(hidden, norm_gain):
    values = hidden.astype(jnp.float32)
    factor = lax.rsqrt(jnp.mean(values * values, axis=-1, keepdims=True) + norm_eps)
    return (values * factor * norm_gain).astype(jnp.bfloat16)


def rotary_embed(values, token_positions):
    half_width = values.shape[-1] // 2
    frequency = rope_base ** (-jnp.arange(half_width, dtype=jnp.float32) * 2.0 / values.shape[-1])
    angles = token_positions.astype(jnp.float32)[:, None] * frequency[None, :]
    cosine_table = jnp.concatenate([jnp.cos(angles), jnp.cos(angles)], axis=-1)
    sine_table = jnp.concatenate([jnp.sin(angles), jnp.sin(angles)], axis=-1)
    first_half = values[..., :half_width]
    second_half = values[..., half_width:]
    rotated = jnp.concatenate([-second_half, first_half], axis=-1)
    return values * cosine_table + rotated * sine_table


def on_device(
    hidden,
    norm_gain,
    lengths,
    query_param,
    query_grad,
    query_moment,
    query_second,
    keyval_param,
    keyval_gradient,
    keyval_first_moment,
    keyval_second_moment,
    output_param,
    output_grad,
    output_moment,
    output_second,
):
    sections = lax.axis_size("section")
    planes = lax.axis_size("plane")
    lanes = lax.axis_size("lane")
    members = sections * lanes
    group = ("section", "lane")
    rows = query_param.shape[0]
    head_columns = query_param.shape[1] // members
    heads_here = head_columns // HEAD_DIMENSION
    tokens_here, model_width = hidden.shape[1:]
    sequence = tokens_here * planes * lanes

    query_weight = adam_update(query_param, query_grad, query_moment, query_second)
    keyval_matrix = adam_update(
        keyval_param, keyval_gradient, keyval_first_moment, keyval_second_moment
    )
    output_weight = adam_update(output_param, output_grad, output_moment, output_second)

    spread_heads = jnp.repeat(
        keyval_matrix.reshape(rows, 2, KEYVAL_HEADS, HEAD_DIMENSION),
        members // KEYVAL_HEADS,
        axis=2,
    )
    spread_heads = spread_heads.transpose(2, 0, 1, 3).reshape(members, rows, 2 * HEAD_DIMENSION)
    query_pieces = query_weight.reshape(rows, members, head_columns).transpose(1, 0, 2)
    output_pieces = output_weight.reshape(rows, members, head_columns).transpose(1, 0, 2)
    query_rows = lax.all_to_all(query_pieces, group, 0, 0, tiled=True)
    keyval_rows = lax.all_to_all(spread_heads, group, 0, 0, tiled=True)
    output_rows = lax.all_to_all(output_pieces, group, 0, 0, tiled=True)
    query_rows = query_rows.reshape(members * rows, head_columns)
    keyval_rows = keyval_rows.reshape(members * rows, 2 * HEAD_DIMENSION)
    output_rows = output_rows.reshape(members * rows, head_columns)

    local_rows = normalize(hidden[0], norm_gain)
    features = local_rows.reshape(tokens_here, sections, planes, lanes * rows)
    features = features.transpose(2, 0, 1, 3).reshape(planes, tokens_here, members * rows)
    features = lax.all_to_all(features, "plane", 0, 0, tiled=True)
    normed = lax.all_gather(features, group, axis=0, tiled=True)
    normed = normed.reshape(sections * sequence, members * rows)

    partial = jnp.concatenate(
        [
            jnp.dot(normed, query_rows, preferred_element_type=jnp.float32).astype(jnp.bfloat16),
            jnp.dot(normed, keyval_rows, preferred_element_type=jnp.float32).astype(jnp.bfloat16),
        ],
        axis=1,
    ).reshape(sections, sequence, head_columns + 2 * HEAD_DIMENSION)
    partial = lax.all_to_all(partial, "plane", 0, 0, tiled=True)
    total = jnp.sum(partial.astype(jnp.float32), axis=0)

    order = jnp.arange(sequence).reshape(planes, lanes, tokens_here)
    token_positions = order.transpose(1, 0, 2).reshape(sequence)
    length = lax.dynamic_index_in_dim(
        lax.all_gather(lengths, "section", axis=0, tiled=True), lax.axis_index("plane"), 0, False
    )
    query_heads = rotary_embed(
        total[:, :head_columns].reshape(sequence, heads_here, HEAD_DIMENSION).transpose(1, 0, 2),
        token_positions,
    ).astype(jnp.bfloat16)
    key_head_rows = rotary_embed(
        total[:, head_columns : head_columns + HEAD_DIMENSION], token_positions
    ).astype(jnp.bfloat16)
    value_head_rows = total[:, head_columns + HEAD_DIMENSION :].astype(jnp.bfloat16)
    scores = jnp.einsum(
        "hqd,kd->hqk", query_heads, key_head_rows, preferred_element_type=jnp.float32
    ) / math.sqrt(HEAD_DIMENSION)
    allowed = (token_positions[None, :] <= token_positions[:, None]) & (
        token_positions[None, :] < length
    )
    scores = jnp.where(allowed[None], scores, masked_score)
    row_max = jnp.max(scores, axis=-1, keepdims=True)
    exponent = jnp.exp(scores - row_max)
    attention = (exponent / jnp.sum(exponent, axis=-1, keepdims=True)).astype(jnp.bfloat16)
    head_out = jnp.einsum(
        "hqk,kd->hqd", attention, value_head_rows, preferred_element_type=jnp.float32
    ).astype(jnp.bfloat16)
    head_out = head_out.transpose(1, 0, 2).reshape(sequence, head_columns)

    all_heads = lax.all_gather(head_out, "plane", axis=0, tiled=True)
    feature_part = lax.dot_general(
        all_heads, output_rows, (((1,), (1,)), ((), ())), preferred_element_type=jnp.float32
    ).astype(jnp.bfloat16)
    feature_part = feature_part.reshape(members, planes * tokens_here, members * rows)
    feature_part = lax.all_to_all(feature_part, group, 0, 0, tiled=True)
    summed = jnp.sum(feature_part.astype(jnp.float32), axis=0).astype(jnp.bfloat16)
    arrived = lax.all_to_all(
        summed.reshape(planes, tokens_here, members * rows), "plane", 0, 0, tiled=True
    )
    ordered = arrived.reshape(planes, tokens_here, sections, lanes * rows).transpose(1, 2, 0, 3)
    return ordered.reshape(1, tokens_here, model_width)


def rope_tables(positions):
    half_width = HEAD_DIMENSION // 2
    frequency = (
        rope_base ** (-np.arange(half_width, dtype=np.float64) * 2.0 / HEAD_DIMENSION)
    ).astype(np.float32)
    angles = positions.astype(np.float32)[:, None] * frequency[None, :]
    cosine, sine = np.cos(angles), np.sin(angles)
    return (
        np.concatenate([cosine, cosine], axis=-1).astype(np.float32),
        np.concatenate([-sine, sine], axis=-1).astype(np.float32),
    )


def block_kernel(
    sizes,
    hidden,
    norm_gain,
    lengths,
    cosine,
    sine,
    qp,
    qg,
    qm,
    qs,
    kp,
    kg,
    km,
    ks,
    op,
    og,
    om,
    os_,
    out,
    fetched,
    a_send,
    a_all,
    w_send,
    w_all,
    o_send,
    o_all,
    x_send,
    normed,
    pa_send,
    pa_recv,
    pb_send,
    pb_recv,
    total_a,
    total_b,
    keyval,
    heads_a,
    heads_b,
    pair_send,
    pair_recv,
    red_send,
    red_recv,
    z_send,
    z_recv,
    length,
    length_here,
    fetch_sem,
    local_sem,
    a_ssem,
    a_rsem,
    w_ssem,
    w_rsem,
    o_ssem,
    o_rsem,
    x_ssem,
    x_rsem,
    g_ssem,
    g_rsem,
    d_ssem,
    d_rsem,
    f_ssem,
    pa_ssem,
    pa_rsem,
    pb_ssem,
    pb_rsem,
    k_ssem,
    k_rsem,
    ha_ssem,
    ha_rsem,
    hb_ssem,
    hb_rsem,
    b_ssem,
    b_rsem,
    r_ssem,
    r_rsem,
    z_ssem,
    z_rsem,
    l_ssem,
    l_rsem,
):
    S, NP, L = sizes
    G = S * L
    half = S // 2
    s, p, l = lax.axis_index("section"), lax.axis_index("plane"), lax.axis_index("lane")
    j = s * L + l
    core = lax.rem(s, 2)
    pair = s // 2
    sibling = s + 1 - 2 * core
    rows = qp.shape[0]
    split = w_all.shape[2]
    first = a_all.shape[2] - HEAD_DIMENSION
    hc = first + split
    tokens = hidden.shape[0]
    strip = L * rows
    seq = NP * tokens * L

    def member(m):
        return (m // L, p, lax.rem(m, L))

    def at_plane(q):
        return (s, q, l)

    def remote(src, dst, ssem, rsem, device):
        return pltpu.make_async_remote_copy(
            src_ref=src,
            dst_ref=dst,
            send_sem=ssem,
            recv_sem=rsem,
            device_id=device,
            device_id_type=pl.DeviceIdType.MESH,
        )

    def section_of(plane):
        core_of = lax.rem(plane, 2)
        return 2 * lax.rem(plane // 2 + core_of, half) + core_of

    kept = section_of(p)

    same_core = []
    for da in range(half):
        for dl in range(L):
            sec = 2 * lax.rem(pair + da, half) + core
            lane = lax.rem(l + dl, L)
            same_core.append((sec, lane))
    others = same_core[1:]

    length[...] = jnp.full(length.shape, lengths[0], jnp.int32)

    barrier = pltpu.get_barrier_semaphore()
    for d in range(1, G):
        pl.semaphore_signal(
            barrier, inc=1, device_id=member(lax.rem(j + d, G)), device_id_type=pl.DeviceIdType.MESH
        )
    for d in range(1, NP):
        pl.semaphore_signal(
            barrier,
            inc=1,
            device_id=at_plane(lax.rem(p + d, NP)),
            device_id_type=pl.DeviceIdType.MESH,
        )

    def fetch(refs, kv_refs, begin, n_columns, i, slot):
        dest = lax.rem(j + i, G)
        sec, lane = dest // L, lax.rem(dest, L)
        chip = (sec // 2) * L + lane
        block = chip * 2 + lax.rem(sec, 2)
        copies = []
        for a, ref in enumerate(refs):
            copies.append(
                pltpu.make_async_copy(
                    ref.at[:, pl.ds(pl.multiple_of(block * hc + begin, 128), n_columns)],
                    fetched.at[slot, a, :, pl.ds(0, n_columns)],
                    fetch_sem.at[slot, a, 0],
                )
            )
        for a, ref in enumerate(kv_refs):
            head = lax.rem(sec, 2) * KEYVAL_HEADS + chip
            copies.append(
                pltpu.make_async_copy(
                    ref.at[:, pl.ds(pl.multiple_of(head * HEAD_DIMENSION, 128), HEAD_DIMENSION)],
                    fetched.at[slot, a, :, pl.ds(n_columns, HEAD_DIMENSION)],
                    fetch_sem.at[slot, a, 1],
                )
            )
        return copies

    def update_all(job, following, n_columns, dst, after):
        @pl.loop(1, G + 1)
        def _(i):
            slot = lax.rem(i, 2)
            for copy in fetch(*job, i, slot):
                copy.wait()

            @pl.when(i < G)
            def _():
                for copy in fetch(*job, i + 1, 1 - slot):
                    copy.start()

            if following is not None:

                @pl.when(i == G)
                def _():
                    for copy in fetch(*following, 1, 1):
                        copy.start()

            @pl.loop(0, rows // 16)
            def _(t):
                r = pl.ds(pl.multiple_of(t * 16, 16), 16)
                piece = [fetched[slot, a, r, 0:n_columns] for a in range(4)]
                dst[i - 1, r, :] = adam_update(*piece)

            after(i)

    query_refs, keyval_refs = (qp, qg, qm, qs), (kp, kg, km, ks)
    job_a = (query_refs, keyval_refs, 0, first)
    job_w = (query_refs, (), first, split)
    job_o = ((op, og, om, os_), (), 0, hc)
    for copy in fetch(*job_a, 1, 1):
        copy.start()

    squares = jnp.zeros((tokens, 1), jnp.float32)
    for c in range(S * NP):
        v = hidden[:, c * strip : (c + 1) * strip].astype(jnp.float32)
        squares += jnp.sum(v * v, axis=-1, keepdims=True)
    factor = lax.rsqrt(squares / (S * NP * strip) + norm_eps)
    for c in range(S * NP):
        at = slice(c * strip, (c + 1) * strip)
        v = hidden[:, at].astype(jnp.float32) * factor * norm_gain[0:1, at]
        x_send[c % NP, :, (c // NP) * strip : (c // NP + 1) * strip] = v.astype(jnp.bfloat16)

    pl.semaphore_wait(barrier, G - 1 + NP - 1)

    @pl.when(s == kept)
    def _():
        for d in range(1, S):
            remote(
                length, length_here, l_ssem.at[d], l_rsem, (lax.rem(s + d, S), p, l)
            ).start()

    def x_copy(q, src_plane, d):
        return remote(
            x_send.at[q], normed.at[j, src_plane], x_ssem.at[d], x_rsem.at[src_plane], at_plane(q)
        )

    for d in range(1, NP):
        x_copy(lax.rem(p + d, NP), p, d).start()
    own_x = pltpu.make_async_copy(x_send.at[p], normed.at[j, p], local_sem.at[0])
    own_x.start()

    def weight_copies(send, gathered, ssem, rsem):
        def copy(i):
            return remote(
                send.at[i - 1],
                gathered.at[j],
                ssem.at[i - 1],
                rsem.at[j],
                member(lax.rem(j + i, G)),
            )

        return copy

    def weight_wait(send, gathered, ssem, rsem):
        for d in range(1, G):
            src = lax.rem(j + d, G)
            remote(
                send.at[0], gathered.at[src], ssem.at[0], rsem.at[src], member(src)
            ).wait_recv()

    a_copy = weight_copies(a_send, a_all, a_ssem, a_rsem)
    w_copy = weight_copies(w_send, w_all, w_ssem, w_rsem)
    o_copy = weight_copies(o_send, o_all, o_ssem, o_rsem)

    def after_a(i):
        @pl.when(i < G)
        def _():
            a_copy(i).start()

    update_all(job_a, job_w, first + HEAD_DIMENSION, a_send, after_a)
    own_a = pltpu.make_async_copy(a_send.at[G - 1], a_all.at[j], local_sem.at[1])
    own_a.start()
    update_all(job_w, job_o, split, w_send, lambda i: None)
    own_w = pltpu.make_async_copy(w_send.at[G - 1], w_all.at[j], local_sem.at[2])
    own_w.start()

    for d in range(1, NP):
        src_plane = lax.rem(p + d, NP)
        remote(
            x_send.at[src_plane],
            normed.at[j, src_plane],
            x_ssem.at[d],
            x_rsem.at[src_plane],
            at_plane(src_plane),
        ).wait_recv()
    own_x.wait()

    def g_copy(block, ssem, device):
        return remote(normed.at[block], normed.at[block], ssem, g_rsem.at[block], device)

    by_lane, by_section, corner = others
    lane_block, section_block, corner_block = (sec * L + lane for sec, lane in others)
    to_lane, to_section = ((sec, p, lane) for sec, lane in (by_lane, by_section))
    g_copy(j, g_ssem.at[0], to_lane).start()
    g_copy(j, g_ssem.at[1], to_section).start()
    g_copy(j, f_ssem.at[0], (sibling, p, l)).start()

    def corner_copy(block, part, device):
        view = normed.at[block, pl.ds(part * (NP // 2), NP // 2)]
        return remote(view, view, d_ssem.at[part], d_rsem.at[part], device)

    update_all(job_o, None, hc, o_send, lambda i: None)
    own_o = pltpu.make_async_copy(o_send.at[G - 1], o_all.at[j], local_sem.at[3])
    own_o.start()

    g_copy(section_block, g_ssem.at[1], to_section).wait_recv()
    corner_copy(section_block, 0, to_lane).start()
    g_copy(section_block, f_ssem.at[2], (sibling, p, l)).start()
    g_copy(lane_block, g_ssem.at[0], to_lane).wait_recv()
    corner_copy(lane_block, 1, to_section).start()
    g_copy(lane_block, f_ssem.at[1], (sibling, p, l)).start()
    for i in range(1, G):
        w_copy(i).start()
    corner_copy(corner_block, 0, to_lane).wait_recv()
    corner_copy(corner_block, 1, to_section).wait_recv()
    g_copy(corner_block, f_ssem.at[3], (sibling, p, l)).start()
    weight_wait(a_send, a_all, a_ssem, a_rsem)
    own_a.wait()
    for n, (sec, lane) in enumerate(same_core):
        block = (sec + 1 - 2 * core) * L + lane
        g_copy(block, f_ssem.at[n], (sibling, p, l)).wait_recv()

    def product(plane, weight):
        x = normed[pl.ds(section_of(plane) * L, L)].reshape(seq, G * rows)
        w = weight[...].reshape(G * rows, weight.shape[2])
        return jnp.dot(x, w, preferred_element_type=jnp.float32)

    def part_copy(send, recv, ssem, rsem, d):
        q = lax.rem(p + d, NP)
        return remote(send.at[d - 1], recv.at[p], ssem.at[d - 1], rsem.at[p], at_plane(q))

    def spread(weight, send, recv, ssem, rsem, own):
        @pl.loop(1, NP)
        def _(d):
            send[d - 1] = product(lax.rem(p + d, NP), weight).astype(jnp.bfloat16)
            part_copy(send, recv, ssem, rsem, d).start()

        own[...] = product(p, weight)

    def collect(send, recv, ssem, rsem, own):
        for d in range(1, NP):
            q = lax.rem(p + d, NP)
            remote(send.at[0], recv.at[q], ssem.at[0], rsem.at[q], at_plane(q)).wait_recv()
            own[...] += recv[q].astype(jnp.float32)

    spread(a_all, pa_send, pa_recv, pa_ssem, pa_rsem, total_a)
    weight_wait(w_send, w_all, w_ssem, w_rsem)
    own_w.wait()
    for i in range(1, G):
        o_copy(i).start()
    spread(w_all, pb_send, pb_recv, pb_ssem, pb_rsem, total_b)
    collect(pa_send, pa_recv, pa_ssem, pa_rsem, total_a)

    @pl.when(s == kept)
    def _():
        length_here[...] = length[...]
        for d in range(1, S):
            remote(
                length, length_here, l_ssem.at[d], l_rsem, (lax.rem(s + d, S), p, l)
            ).wait_send()

    @pl.when(s != kept)
    def _():
        remote(length, length_here, l_ssem.at[0], l_rsem, (kept, p, l)).wait_recv()

    def rotate(x):
        return (x * cosine[...] + pltpu.roll(x, HEAD_DIMENSION // 2, 1) * sine[...]).astype(
            jnp.bfloat16
        )

    raw = total_a[:, first:]
    keyval[core] = jnp.where(core == 0, rotate(raw), raw.astype(jnp.bfloat16))

    def k_copy(index):
        return remote(keyval.at[index], keyval.at[index], k_ssem, k_rsem, (sibling, p, l))

    k_copy(core).start()

    def positions(index):
        place = index
        for block in range(1, L * NP):
            here, before = (
                ((b % NP) * L + b // NP) * tokens - b * tokens for b in (block, block - 1)
            )
            place += jnp.where(index >= block * tokens, here - before, 0)
        return place

    column = positions(lax.broadcasted_iota(jnp.int32, (1, seq), 1))
    row = positions(lax.broadcasted_iota(jnp.int32, (seq, 1), 0))
    limit = jnp.concatenate([length_here[0:1, :]] * (seq // 128), axis=1)
    allowed = (column <= row) & (column < limit)
    k_copy(1 - core).wait_recv()

    def attend(own, n_columns, gathered):
        for h in range(n_columns // HEAD_DIMENSION):
            at = slice(h * HEAD_DIMENSION, (h + 1) * HEAD_DIMENSION)
            scores = lax.dot_general(
                rotate(own[:, at]),
                keyval[0],
                (((1,), (1,)), ((), ())),
                preferred_element_type=jnp.float32,
            ) / math.sqrt(HEAD_DIMENSION)
            scores = jnp.where(allowed, scores, masked_score)
            exponent = jnp.exp(scores - jnp.max(scores, axis=-1, keepdims=True))
            attention = exponent / jnp.sum(exponent, axis=-1, keepdims=True)
            gathered[p, :, at] = jnp.dot(
                attention.astype(jnp.bfloat16), keyval[1], preferred_element_type=jnp.float32
            ).astype(jnp.bfloat16)

    def head_copy(gathered, ssem, rsem, d):
        return remote(
            gathered.at[p], gathered.at[p], ssem.at[d], rsem.at[p], at_plane(lax.rem(p + d, NP))
        )

    attend(total_a, first, heads_a)
    for d in range(1, NP):
        head_copy(heads_a, ha_ssem, ha_rsem, d).start()
    collect(pb_send, pb_recv, pb_ssem, pb_rsem, total_b)
    attend(total_b, split, heads_b)
    for d in range(1, NP):
        head_copy(heads_b, hb_ssem, hb_rsem, d).start()

    weight_wait(o_send, o_all, o_ssem, o_rsem)
    own_o.wait()

    def heads_wait(q):
        @pl.when(q != p)
        def _():
            for gathered, ssem, rsem in ((heads_a, ha_ssem, ha_rsem), (heads_b, hb_ssem, hb_rsem)):
                remote(
                    gathered.at[q], gathered.at[q], ssem.at[0], rsem.at[q], at_plane(q)
                ).wait_recv()

    def features(prompt, b):
        over = (((1,), (1,)), ((), ()))
        return lax.dot_general(
            heads_a[prompt], o_all[b, :, 0:first], over, preferred_element_type=jnp.float32
        ) + lax.dot_general(
            heads_b[prompt], o_all[b, :, first:], over, preferred_element_type=jnp.float32
        )

    def b_copy(e, part):
        return remote(
            pair_send.at[e, part],
            pair_recv.at[e, part],
            b_ssem.at[e, part],
            b_rsem.at[e, part],
            (sibling, p, l),
        )

    here = pair * L + l

    def r_copy(e, part, dl, start):
        chip = lax.rem(p // 2 + e + core, half)
        lane = lax.rem(l + dl, L)

        @pl.when((chip * L + lane) != here)
        def _():
            copy = remote(
                red_send.at[e, part, lane],
                red_recv.at[here, part],
                r_ssem.at[e, part, dl],
                r_rsem.at[here, part],
                (2 * chip + core, p, lane),
            )
            if start:
                copy.start()
            else:
                copy.wait_send()

    for e in range(half):
        theirs = 2 * lax.rem(p // 2 + e, half) + 1 - core
        mine = 2 * lax.rem(p // 2 + e, half) + core
        heads_wait(theirs)
        for part in range(2):

            @pl.loop(0, G // 2)
            def _(b):
                at = pl.ds(pl.multiple_of(b * rows, 128), rows)
                value = features(theirs, part * (G // 2) + b)
                pair_send[e, part, :, at] = value.astype(jnp.bfloat16)

            b_copy(e, part).start()
        heads_wait(mine)
        for part in range(2):
            b_copy(e, part).wait_recv()

            @pl.loop(0, G // 2)
            def _(b):
                at = pl.ds(pl.multiple_of(b * rows, 128), rows)
                value = features(mine, part * (G // 2) + b)
                value += pair_recv[e, part, :, at].astype(jnp.float32)
                red_send[e, part, :, :, at] = value.astype(jnp.bfloat16).reshape(
                    L, seq // L, rows
                )

            for dl in range(L):
                r_copy(e, part, dl, True)

    def z_copy(q, part, d):
        return remote(
            z_send.at[part, q],
            z_recv.at[part, p],
            z_ssem.at[part, d],
            z_rsem.at[part, p],
            at_plane(q),
        )

    for part in range(2):
        summed = red_send[lax.rem(pair + 2 * half - core - p // 2, half), part, l].astype(
            jnp.float32
        )
        for sec, lane in others:
            src = (sec // 2) * L + lane
            remote(
                red_send.at[0, part, l],
                red_recv.at[src, part],
                r_ssem.at[0, part, 0],
                r_rsem.at[src, part],
                (sec, p, lane),
            ).wait_recv()
            summed += red_recv[src, part].astype(jnp.float32)
        z_send[part] = summed.astype(jnp.bfloat16).reshape(NP, tokens, G * rows // 2)
        for d in range(1, NP):
            z_copy(lax.rem(p + d, NP), part, d).start()
        z_recv[part, p] = z_send[part, p]
    for part in range(2):
        for d in range(1, NP):
            q = lax.rem(p + d, NP)
            remote(
                z_send.at[part, q],
                z_recv.at[part, q],
                z_ssem.at[part, d],
                z_rsem.at[part, q],
                at_plane(q),
            ).wait_recv()
    for c in range(S * NP):
        sec = c // NP
        at = (sec % half) * strip
        out[:, c * strip : (c + 1) * strip] = z_recv[sec // half, c % NP, :, at : at + strip]

    for d in range(1, NP):
        q = lax.rem(p + d, NP)
        x_copy(q, p, d).wait_send()
        part_copy(pa_send, pa_recv, pa_ssem, pa_rsem, d).wait_send()
        part_copy(pb_send, pb_recv, pb_ssem, pb_rsem, d).wait_send()
        head_copy(heads_a, ha_ssem, ha_rsem, d).wait_send()
        head_copy(heads_b, hb_ssem, hb_rsem, d).wait_send()
        for part in range(2):
            z_copy(q, part, d).wait_send()
    for i in range(1, G):
        a_copy(i).wait_send()
        w_copy(i).wait_send()
        o_copy(i).wait_send()
    g_copy(j, g_ssem.at[0], to_lane).wait_send()
    g_copy(j, g_ssem.at[1], to_section).wait_send()
    corner_copy(section_block, 0, to_lane).wait_send()
    corner_copy(lane_block, 1, to_section).wait_send()
    for n, (sec, lane) in enumerate(same_core):
        g_copy(sec * L + lane, f_ssem.at[n], (sibling, p, l)).wait_send()
    k_copy(core).wait_send()
    for e in range(half):
        for part in range(2):
            b_copy(e, part).wait_send()
            for dl in range(L):
                r_copy(e, part, dl, False)


def fused(hidden, norm_gain, lengths, *weights):
    S, NP, L = (lax.axis_size(a) for a in ("section", "plane", "lane"))
    G = S * L
    half = S // 2
    rows = weights[0].shape[0]
    hc = weights[0].shape[1] // G
    first = hc // 2
    split = hc - first
    width = first + HEAD_DIMENSION
    tokens = hidden.shape[1]
    seq = tokens * NP * L
    order = np.arange(seq).reshape(NP, L, tokens).transpose(1, 0, 2).reshape(seq)
    cosine, sine = rope_tables(order)
    bf, f32 = jnp.bfloat16, jnp.float32
    dma = pltpu.SemaphoreType.DMA
    vmem = pl.BlockSpec(memory_space=pltpu.VMEM)
    hbm = pl.BlockSpec(memory_space=pl.ANY)
    smem = pl.BlockSpec(memory_space=pltpu.SMEM)
    scratch = [
        pltpu.VMEM((2, 4, rows, max(width, hc)), f32),
        pltpu.VMEM((G, rows, width), bf),
        pltpu.VMEM((G, rows, width), bf),
        pltpu.VMEM((G, rows, split), bf),
        pltpu.VMEM((G, rows, split), bf),
        pltpu.VMEM((G, rows, hc), bf),
        pltpu.VMEM((G, rows, hc), bf),
        pltpu.VMEM((NP, tokens, G * rows), bf),
        pltpu.VMEM((G, NP, tokens, G * rows), bf),
        pltpu.VMEM((NP - 1, seq, width), bf),
        pltpu.VMEM((NP, seq, width), bf),
        pltpu.VMEM((NP - 1, seq, split), bf),
        pltpu.VMEM((NP, seq, split), bf),
        pltpu.VMEM((seq, width), f32),
        pltpu.VMEM((seq, split), f32),
        pltpu.VMEM((2, seq, HEAD_DIMENSION), bf),
        pltpu.VMEM((NP, seq, first), bf),
        pltpu.VMEM((NP, seq, split), bf),
        pltpu.VMEM((half, 2, seq, G * rows // 2), bf),
        pltpu.VMEM((half, 2, seq, G * rows // 2), bf),
        pltpu.VMEM((half, 2, L, seq // L, G * rows // 2), bf),
        pltpu.VMEM((half * L, 2, seq // L, G * rows // 2), bf),
        pltpu.VMEM((2, NP, tokens, G * rows // 2), bf),
        pltpu.VMEM((2, NP, tokens, G * rows // 2), bf),
        pltpu.VMEM((8, 128), jnp.int32),
        pltpu.VMEM((8, 128), jnp.int32),
        dma((2, 4, 2)),
        dma((4,)),
    ]
    scratch += [dma((G,))] * 6
    scratch += [dma((NP,))] * 2
    scratch += [dma((half * L,)), dma((G,)), dma((2,)), dma((2,)), dma((half * L,))]
    scratch += [dma((NP,))] * 4
    scratch += [dma, dma]
    scratch += [dma((NP,))] * 4
    scratch += [dma((half, 2))] * 2
    scratch += [dma((half, 2, L)), dma((half * L, 2))]
    scratch += [dma((2, NP))] * 2
    scratch += [dma((S,)), dma]
    result = pl.pallas_call(
        functools.partial(block_kernel, (S, NP, L)),
        out_shape=jax.ShapeDtypeStruct(hidden.shape[1:], bf),
        in_specs=[vmem, vmem, smem, vmem, vmem] + [hbm] * 12,
        out_specs=vmem,
        scratch_shapes=scratch,
        compiler_params=pltpu.CompilerParams(
            collective_id=0, has_side_effects=True, vmem_limit_bytes=58 * 2**20
        ),
        cost_estimate=pl.CostEstimate(
            flops=8 * 10**9, bytes_accessed=4 * 10**7, transcendentals=10**6
        ),
    )(
        hidden[0],
        norm_gain[None, :],
        lengths,
        jnp.asarray(cosine),
        jnp.asarray(sine),
        *weights,
    )
    return result[None]


def layer(hidden, norm_gain, lengths, *weights):
    whole_tiles = (
        hidden.shape[1] % 16 == 0
        and weights[0].shape[0] % 128 == 0
        and lax.axis_size("section") % 2 == 0
        and lax.axis_size("section") * lax.axis_size("lane") == 2 * KEYVAL_HEADS
        and lax.axis_size("section") == 2 * lax.axis_size("lane")
        and lax.axis_size("plane") % 2 == 0
        and weights[0].shape[1] % (4 * HEAD_DIMENSION * KEYVAL_HEADS) == 0
    )
    return (fused if whole_tiles else on_device)(hidden, norm_gain, lengths, *weights)


def solution(mesh):
    sections, tensors = mesh.shape["section"], mesh.shape["tensor"]
    lanes = tensors // sections
    grid = Mesh(
        mesh.devices.reshape(sections, tensors // lanes, lanes), ("section", "plane", "lane")
    )
    row_spec = P(("section", "plane", "lane"), None)
    token_spec = P("section", ("plane", "lane"), None)
    return jax.shard_map(
        layer,
        mesh=grid,
        in_specs=(token_spec, P(), P("section")) + (row_spec,) * 12,
        out_specs=token_spec,
        check_vma=False,
    )
```

```python
import functools
import math

import jax
import jax.numpy as jnp
import numpy as np
from jax import lax
from jax.experimental import pallas as pl
from jax.experimental.pallas import tpu as pltpu
from jax.sharding import Mesh, PartitionSpec as P

QUERY_HEADS_LOCAL = 32
KEYVAL_HEADS = 4
HEAD_DIMENSION = 128


learn_rate = 0.015
beta_one = 0.5
beta_two = 0.9
adam_step = 1000.0
adam_eps = 1e-08
decay_rate = 0.1
norm_eps = 1e-06
rope_base = 1000000.0
masked_score = -1e30


def adam_update(current, gradient, moment, second):
    moment_new = beta_one * moment + (1.0 - beta_one) * gradient
    second_new = beta_two * second + (1.0 - beta_two) * gradient * gradient
    corrected = moment_new / (1.0 - beta_one**adam_step)
    denominator = jnp.sqrt(second_new / (1.0 - beta_two**adam_step)) + adam_eps
    return (current - learn_rate * (corrected / denominator + decay_rate * current)).astype(
        jnp.bfloat16
    )


def normalize(hidden, norm_gain):
    values = hidden.astype(jnp.float32)
    factor = lax.rsqrt(jnp.mean(values * values, axis=-1, keepdims=True) + norm_eps)
    return (values * factor * norm_gain).astype(jnp.bfloat16)


def rotary_embed(values, token_positions):
    half_width = values.shape[-1] // 2
    frequency = rope_base ** (-jnp.arange(half_width, dtype=jnp.float32) * 2.0 / values.shape[-1])
    angles = token_positions.astype(jnp.float32)[:, None] * frequency[None, :]
    cosine_table = jnp.concatenate([jnp.cos(angles), jnp.cos(angles)], axis=-1)
    sine_table = jnp.concatenate([jnp.sin(angles), jnp.sin(angles)], axis=-1)
    first_half = values[..., :half_width]
    second_half = values[..., half_width:]
    rotated = jnp.concatenate([-second_half, first_half], axis=-1)
    return values * cosine_table + rotated * sine_table


def on_device(
    hidden,
    norm_gain,
    lengths,
    query_param,
    query_grad,
    query_moment,
    query_second,
    keyval_param,
    keyval_gradient,
    keyval_first_moment,
    keyval_second_moment,
    output_param,
    output_grad,
    output_moment,
    output_second,
):
    sections = lax.axis_size("section")
    planes = lax.axis_size("plane")
    lanes = lax.axis_size("lane")
    members = sections * lanes
    group = ("section", "lane")
    rows = query_param.shape[0]
    head_columns = query_param.shape[1] // members
    heads_here = head_columns // HEAD_DIMENSION
    tokens_here, model_width = hidden.shape[1:]
    sequence = tokens_here * planes * lanes

    query_weight = adam_update(query_param, query_grad, query_moment, query_second)
    keyval_matrix = adam_update(
        keyval_param, keyval_gradient, keyval_first_moment, keyval_second_moment
    )
    output_weight = adam_update(output_param, output_grad, output_moment, output_second)

    spread_heads = jnp.repeat(
        keyval_matrix.reshape(rows, 2, KEYVAL_HEADS, HEAD_DIMENSION),
        members // KEYVAL_HEADS,
        axis=2,
    )
    spread_heads = spread_heads.transpose(2, 0, 1, 3).reshape(members, rows, 2 * HEAD_DIMENSION)
    query_pieces = query_weight.reshape(rows, members, head_columns).transpose(1, 0, 2)
    output_pieces = output_weight.reshape(rows, members, head_columns).transpose(1, 0, 2)
    query_rows = lax.all_to_all(query_pieces, group, 0, 0, tiled=True)
    keyval_rows = lax.all_to_all(spread_heads, group, 0, 0, tiled=True)
    output_rows = lax.all_to_all(output_pieces, group, 0, 0, tiled=True)
    query_rows = query_rows.reshape(members * rows, head_columns)
    keyval_rows = keyval_rows.reshape(members * rows, 2 * HEAD_DIMENSION)
    output_rows = output_rows.reshape(members * rows, head_columns)

    local_rows = normalize(hidden[0], norm_gain)
    features = local_rows.reshape(tokens_here, sections, planes, lanes * rows)
    features = features.transpose(2, 0, 1, 3).reshape(planes, tokens_here, members * rows)
    features = lax.all_to_all(features, "plane", 0, 0, tiled=True)
    normed = lax.all_gather(features, group, axis=0, tiled=True)
    normed = normed.reshape(sections * sequence, members * rows)

    partial = jnp.concatenate(
        [
            jnp.dot(normed, query_rows, preferred_element_type=jnp.float32).astype(jnp.bfloat16),
            jnp.dot(normed, keyval_rows, preferred_element_type=jnp.float32).astype(jnp.bfloat16),
        ],
        axis=1,
    ).reshape(sections, sequence, head_columns + 2 * HEAD_DIMENSION)
    partial = lax.all_to_all(partial, "plane", 0, 0, tiled=True)
    total = jnp.sum(partial.astype(jnp.float32), axis=0)

    order = jnp.arange(sequence).reshape(planes, lanes, tokens_here)
    token_positions = order.transpose(1, 0, 2).reshape(sequence)
    length = lax.dynamic_index_in_dim(
        lax.all_gather(lengths, "section", axis=0, tiled=True), lax.axis_index("plane"), 0, False
    )
    query_heads = rotary_embed(
        total[:, :head_columns].reshape(sequence, heads_here, HEAD_DIMENSION).transpose(1, 0, 2),
        token_positions,
    ).astype(jnp.bfloat16)
    key_head_rows = rotary_embed(
        total[:, head_columns : head_columns + HEAD_DIMENSION], token_positions
    ).astype(jnp.bfloat16)
    value_head_rows = total[:, head_columns + HEAD_DIMENSION :].astype(jnp.bfloat16)
    scores = jnp.einsum(
        "hqd,kd->hqk", query_heads, key_head_rows, preferred_element_type=jnp.float32
    ) / math.sqrt(HEAD_DIMENSION)
    allowed = (token_positions[None, :] <= token_positions[:, None]) & (
        token_positions[None, :] < length
    )
    scores = jnp.where(allowed[None], scores, masked_score)
    row_max = jnp.max(scores, axis=-1, keepdims=True)
    exponent = jnp.exp(scores - row_max)
    attention = (exponent / jnp.sum(exponent, axis=-1, keepdims=True)).astype(jnp.bfloat16)
    head_out = jnp.einsum(
        "hqk,kd->hqd", attention, value_head_rows, preferred_element_type=jnp.float32
    ).astype(jnp.bfloat16)
    head_out = head_out.transpose(1, 0, 2).reshape(sequence, head_columns)

    all_heads = lax.all_gather(head_out, "plane", axis=0, tiled=True)
    feature_part = lax.dot_general(
        all_heads, output_rows, (((1,), (1,)), ((), ())), preferred_element_type=jnp.float32
    ).astype(jnp.bfloat16)
    feature_part = feature_part.reshape(members, planes * tokens_here, members * rows)
    feature_part = lax.all_to_all(feature_part, group, 0, 0, tiled=True)
    summed = jnp.sum(feature_part.astype(jnp.float32), axis=0).astype(jnp.bfloat16)
    arrived = lax.all_to_all(
        summed.reshape(planes, tokens_here, members * rows), "plane", 0, 0, tiled=True
    )
    ordered = arrived.reshape(planes, tokens_here, sections, lanes * rows).transpose(1, 2, 0, 3)
    return ordered.reshape(1, tokens_here, model_width)


def rope_tables(positions):
    half_width = HEAD_DIMENSION // 2
    frequency = (
        rope_base ** (-np.arange(half_width, dtype=np.float64) * 2.0 / HEAD_DIMENSION)
    ).astype(np.float32)
    angles = positions.astype(np.float32)[:, None] * frequency[None, :]
    cosine, sine = np.cos(angles), np.sin(angles)
    return (
        np.concatenate([cosine, cosine], axis=-1).astype(np.float32),
        np.concatenate([-sine, sine], axis=-1).astype(np.float32),
    )


def block_kernel(
    sizes,
    hidden,
    norm_gain,
    lengths,
    cosine,
    sine,
    qp,
    qg,
    qm,
    qs,
    kp,
    kg,
    km,
    ks,
    op,
    og,
    om,
    os_,
    out,
    fetched,
    a_send,
    a_all,
    w_send,
    w_all,
    o_send,
    o_all,
    x_send,
    normed,
    pa_send,
    pa_recv,
    pb_send,
    pb_recv,
    total_a,
    total_b,
    keyval,
    heads_a,
    heads_b,
    pair_send,
    pair_recv,
    red_send,
    red_recv,
    z_send,
    z_recv,
    length,
    length_here,
    fetch_sem,
    local_sem,
    a_ssem,
    a_rsem,
    w_ssem,
    w_rsem,
    o_ssem,
    o_rsem,
    x_ssem,
    x_rsem,
    g_ssem,
    g_rsem,
    d_ssem,
    d_rsem,
    f_ssem,
    pa_ssem,
    pa_rsem,
    pb_ssem,
    pb_rsem,
    k_ssem,
    k_rsem,
    ha_ssem,
    ha_rsem,
    hb_ssem,
    hb_rsem,
    b_ssem,
    b_rsem,
    r_ssem,
    r_rsem,
    z_ssem,
    z_rsem,
    l_ssem,
    l_rsem,
):
    S, NP, L = sizes
    G = S * L
    half = S // 2
    s, p, l = lax.axis_index("section"), lax.axis_index("plane"), lax.axis_index("lane")
    j = s * L + l
    core = lax.rem(s, 2)
    pair = s // 2
    sibling = s + 1 - 2 * core
    rows = qp.shape[0]
    split = w_all.shape[2]
    first = a_all.shape[2] - HEAD_DIMENSION
    hc = first + split
    tokens = hidden.shape[0]
    strip = L * rows
    parts = S
    seq = NP * tokens * L

    def member(m):
        return (m // L, p, lax.rem(m, L))

    def at_plane(q):
        return (s, q, l)

    def remote(src, dst, ssem, rsem, device):
        return pltpu.make_async_remote_copy(
            src_ref=src,
            dst_ref=dst,
            send_sem=ssem,
            recv_sem=rsem,
            device_id=device,
            device_id_type=pl.DeviceIdType.MESH,
        )

    def section_of(plane):
        core_of = lax.rem(plane, 2)
        return 2 * lax.rem(plane // 2 + core_of, half) + core_of

    kept = section_of(p)

    same_core = []
    for da in range(half):
        for dl in range(L):
            sec = 2 * lax.rem(pair + da, half) + core
            lane = lax.rem(l + dl, L)
            same_core.append((sec, lane))
    others = same_core[1:]

    length[...] = jnp.full(length.shape, lengths[0], jnp.int32)

    barrier = pltpu.get_barrier_semaphore()
    for d in range(1, G):
        pl.semaphore_signal(
            barrier, inc=1, device_id=member(lax.rem(j + d, G)), device_id_type=pl.DeviceIdType.MESH
        )
    for d in range(1, NP):
        pl.semaphore_signal(
            barrier,
            inc=1,
            device_id=at_plane(lax.rem(p + d, NP)),
            device_id_type=pl.DeviceIdType.MESH,
        )

    def fetch(refs, kv_refs, begin, n_columns, i, slot):
        dest = lax.rem(j + i, G)
        sec, lane = dest // L, lax.rem(dest, L)
        chip = (sec // 2) * L + lane
        block = chip * 2 + lax.rem(sec, 2)
        copies = []
        for a, ref in enumerate(refs):
            copies.append(
                pltpu.make_async_copy(
                    ref.at[:, pl.ds(pl.multiple_of(block * hc + begin, 128), n_columns)],
                    fetched.at[slot, a, :, pl.ds(0, n_columns)],
                    fetch_sem.at[slot, a, 0],
                )
            )
        for a, ref in enumerate(kv_refs):
            head = lax.rem(sec, 2) * KEYVAL_HEADS + chip
            copies.append(
                pltpu.make_async_copy(
                    ref.at[:, pl.ds(pl.multiple_of(head * HEAD_DIMENSION, 128), HEAD_DIMENSION)],
                    fetched.at[slot, a, :, pl.ds(n_columns, HEAD_DIMENSION)],
                    fetch_sem.at[slot, a, 1],
                )
            )
        return copies

    def update_all(job, following, n_columns, dst, after):
        @pl.loop(1, G + 1)
        def _(i):
            slot = lax.rem(i, 2)
            for copy in fetch(*job, i, slot):
                copy.wait()

            @pl.when(i < G)
            def _():
                for copy in fetch(*job, i + 1, 1 - slot):
                    copy.start()

            if following is not None:

                @pl.when(i == G)
                def _():
                    for copy in fetch(*following, 1, 1):
                        copy.start()

            @pl.loop(0, rows // 16)
            def _(t):
                r = pl.ds(pl.multiple_of(t * 16, 16), 16)
                piece = [fetched[slot, a, r, 0:n_columns] for a in range(4)]
                dst[i - 1, r, :] = adam_update(*piece)

            after(i)

    query_refs, keyval_refs = (qp, qg, qm, qs), (kp, kg, km, ks)
    job_a = (query_refs, keyval_refs, 0, first)
    job_w = (query_refs, (), first, split)
    job_o = ((op, og, om, os_), (), 0, hc)
    for copy in fetch(*job_a, 1, 1):
        copy.start()

    squares = jnp.zeros((tokens, 1), jnp.float32)
    for c in range(S * NP):
        v = hidden[:, c * strip : (c + 1) * strip].astype(jnp.float32)
        squares += jnp.sum(v * v, axis=-1, keepdims=True)
    factor = lax.rsqrt(squares / (S * NP * strip) + norm_eps)
    for c in range(S * NP):
        at = slice(c * strip, (c + 1) * strip)
        v = hidden[:, at].astype(jnp.float32) * factor * norm_gain[0:1, at]
        x_send[c % NP, :, (c // NP) * strip : (c // NP + 1) * strip] = v.astype(jnp.bfloat16)

    pl.semaphore_wait(barrier, G - 1 + NP - 1)

    @pl.when(s == kept)
    def _():
        for d in range(1, S):
            remote(
                length, length_here, l_ssem.at[d], l_rsem, (lax.rem(s + d, S), p, l)
            ).start()

    def x_copy(q, src_plane, d):
        return remote(
            x_send.at[q], normed.at[j, src_plane], x_ssem.at[d], x_rsem.at[src_plane], at_plane(q)
        )

    for d in range(1, NP):
        x_copy(lax.rem(p + d, NP), p, d).start()
    own_x = pltpu.make_async_copy(x_send.at[p], normed.at[j, p], local_sem.at[0])
    own_x.start()

    def weight_copies(send, gathered, ssem, rsem):
        def copy(i):
            return remote(
                send.at[i - 1],
                gathered.at[j],
                ssem.at[i - 1],
                rsem.at[j],
                member(lax.rem(j + i, G)),
            )

        return copy

    def weight_wait(send, gathered, ssem, rsem):
        for d in range(1, G):
            src = lax.rem(j + d, G)
            remote(
                send.at[0], gathered.at[src], ssem.at[0], rsem.at[src], member(src)
            ).wait_recv()

    a_copy = weight_copies(a_send, a_all, a_ssem, a_rsem)
    w_copy = weight_copies(w_send, w_all, w_ssem, w_rsem)
    o_copy = weight_copies(o_send, o_all, o_ssem, o_rsem)

    def after_a(i):
        @pl.when(i < G)
        def _():
            a_copy(i).start()

    update_all(job_a, job_w, first + HEAD_DIMENSION, a_send, after_a)
    own_a = pltpu.make_async_copy(a_send.at[G - 1], a_all.at[j], local_sem.at[1])
    own_a.start()
    update_all(job_w, job_o, split, w_send, lambda i: None)
    own_w = pltpu.make_async_copy(w_send.at[G - 1], w_all.at[j], local_sem.at[2])
    own_w.start()

    for d in range(1, NP):
        src_plane = lax.rem(p + d, NP)
        remote(
            x_send.at[src_plane],
            normed.at[j, src_plane],
            x_ssem.at[d],
            x_rsem.at[src_plane],
            at_plane(src_plane),
        ).wait_recv()
    own_x.wait()

    def g_copy(block, ssem, device):
        return remote(normed.at[block], normed.at[block], ssem, g_rsem.at[block], device)

    by_lane, by_section, corner = others
    lane_block, section_block, corner_block = (sec * L + lane for sec, lane in others)
    to_lane, to_section = ((sec, p, lane) for sec, lane in (by_lane, by_section))
    g_copy(j, g_ssem.at[0], to_lane).start()
    g_copy(j, g_ssem.at[1], to_section).start()
    g_copy(j, f_ssem.at[0], (sibling, p, l)).start()

    def corner_copy(block, part, device):
        view = normed.at[block, pl.ds(part * (NP // 2), NP // 2)]
        return remote(view, view, d_ssem.at[part], d_rsem.at[part], device)

    update_all(job_o, None, hc, o_send, lambda i: None)
    own_o = pltpu.make_async_copy(o_send.at[G - 1], o_all.at[j], local_sem.at[3])
    own_o.start()

    g_copy(section_block, g_ssem.at[1], to_section).wait_recv()
    corner_copy(section_block, 0, to_lane).start()
    g_copy(section_block, f_ssem.at[2], (sibling, p, l)).start()
    g_copy(lane_block, g_ssem.at[0], to_lane).wait_recv()
    corner_copy(lane_block, 1, to_section).start()
    g_copy(lane_block, f_ssem.at[1], (sibling, p, l)).start()
    for i in range(1, G):
        w_copy(i).start()
    corner_copy(corner_block, 0, to_lane).wait_recv()
    corner_copy(corner_block, 1, to_section).wait_recv()
    g_copy(corner_block, f_ssem.at[3], (sibling, p, l)).start()
    weight_wait(a_send, a_all, a_ssem, a_rsem)
    own_a.wait()
    for n, (sec, lane) in enumerate(same_core):
        block = (sec + 1 - 2 * core) * L + lane
        g_copy(block, f_ssem.at[n], (sibling, p, l)).wait_recv()

    def product(plane, weight):
        x = normed[pl.ds(section_of(plane) * L, L)].reshape(seq, G * rows)
        w = weight[...].reshape(G * rows, weight.shape[2])
        return jnp.dot(x, w, preferred_element_type=jnp.float32)

    def part_copy(send, recv, ssem, rsem, d):
        q = lax.rem(p + d, NP)
        return remote(send.at[d - 1], recv.at[p], ssem.at[d - 1], rsem.at[p], at_plane(q))

    def spread(weight, send, recv, ssem, rsem, own):
        @pl.loop(1, NP)
        def _(d):
            send[d - 1] = product(lax.rem(p + d, NP), weight).astype(jnp.bfloat16)
            part_copy(send, recv, ssem, rsem, d).start()

        own[...] = product(p, weight)

    def collect(send, recv, ssem, rsem, own):
        for d in range(1, NP):
            q = lax.rem(p + d, NP)
            remote(send.at[0], recv.at[q], ssem.at[0], rsem.at[q], at_plane(q)).wait_recv()
            own[...] += recv[q].astype(jnp.float32)

    spread(a_all, pa_send, pa_recv, pa_ssem, pa_rsem, total_a)
    weight_wait(w_send, w_all, w_ssem, w_rsem)
    own_w.wait()
    for i in range(1, G):
        o_copy(i).start()
    spread(w_all, pb_send, pb_recv, pb_ssem, pb_rsem, total_b)
    collect(pa_send, pa_recv, pa_ssem, pa_rsem, total_a)

    @pl.when(s == kept)
    def _():
        length_here[...] = length[...]
        for d in range(1, S):
            remote(
                length, length_here, l_ssem.at[d], l_rsem, (lax.rem(s + d, S), p, l)
            ).wait_send()

    @pl.when(s != kept)
    def _():
        remote(length, length_here, l_ssem.at[0], l_rsem, (kept, p, l)).wait_recv()

    def rotate(x):
        return (x * cosine[...] + pltpu.roll(x, HEAD_DIMENSION // 2, 1) * sine[...]).astype(
            jnp.bfloat16
        )

    raw = total_a[:, first:]
    keyval[core] = jnp.where(core == 0, rotate(raw), raw.astype(jnp.bfloat16))

    def k_copy(index):
        return remote(keyval.at[index], keyval.at[index], k_ssem, k_rsem, (sibling, p, l))

    k_copy(core).start()

    def positions(index):
        place = index
        for block in range(1, L * NP):
            here, before = (
                ((b % NP) * L + b // NP) * tokens - b * tokens for b in (block, block - 1)
            )
            place += jnp.where(index >= block * tokens, here - before, 0)
        return place

    column = positions(lax.broadcasted_iota(jnp.int32, (1, seq), 1))
    row = positions(lax.broadcasted_iota(jnp.int32, (seq, 1), 0))
    limit = jnp.concatenate([length_here[0:1, :]] * (seq // 128), axis=1)
    allowed = (column <= row) & (column < limit)
    k_copy(1 - core).wait_recv()

    def attend(own, n_columns, gathered):
        for h in range(n_columns // HEAD_DIMENSION):
            at = slice(h * HEAD_DIMENSION, (h + 1) * HEAD_DIMENSION)
            scores = lax.dot_general(
                rotate(own[:, at]),
                keyval[0],
                (((1,), (1,)), ((), ())),
                preferred_element_type=jnp.float32,
            ) / math.sqrt(HEAD_DIMENSION)
            scores = jnp.where(allowed, scores, masked_score)
            exponent = jnp.exp(scores - jnp.max(scores, axis=-1, keepdims=True))
            attention = exponent / jnp.sum(exponent, axis=-1, keepdims=True)
            gathered[p, :, at] = jnp.dot(
                attention.astype(jnp.bfloat16), keyval[1], preferred_element_type=jnp.float32
            ).astype(jnp.bfloat16)

    def head_copy(gathered, ssem, rsem, d):
        return remote(
            gathered.at[p], gathered.at[p], ssem.at[d], rsem.at[p], at_plane(lax.rem(p + d, NP))
        )

    attend(total_a, first, heads_a)
    for d in range(1, NP):
        head_copy(heads_a, ha_ssem, ha_rsem, d).start()
    collect(pb_send, pb_recv, pb_ssem, pb_rsem, total_b)
    attend(total_b, split, heads_b)
    for d in range(1, NP):
        head_copy(heads_b, hb_ssem, hb_rsem, d).start()

    weight_wait(o_send, o_all, o_ssem, o_rsem)
    own_o.wait()

    def heads_wait(q):
        @pl.when(q != p)
        def _():
            for gathered, ssem, rsem in ((heads_a, ha_ssem, ha_rsem), (heads_b, hb_ssem, hb_rsem)):
                remote(
                    gathered.at[q], gathered.at[q], ssem.at[0], rsem.at[q], at_plane(q)
                ).wait_recv()

    def features(prompt, b):
        over = (((1,), (1,)), ((), ()))
        return lax.dot_general(
            heads_a[prompt], o_all[b, :, 0:first], over, preferred_element_type=jnp.float32
        ) + lax.dot_general(
            heads_b[prompt], o_all[b, :, first:], over, preferred_element_type=jnp.float32
        )

    def b_copy(e, part):
        return remote(
            pair_send.at[e, part],
            pair_recv.at[e, part],
            b_ssem.at[e, part],
            b_rsem.at[e, part],
            (sibling, p, l),
        )

    here = pair * L + l

    def r_copy(e, part, dl, start):
        chip = lax.rem(p // 2 + e + core, half)
        lane = lax.rem(l + dl, L)

        @pl.when((chip * L + lane) != here)
        def _():
            copy = remote(
                red_send.at[e, part, lane],
                red_recv.at[here, part],
                r_ssem.at[e, part, dl],
                r_rsem.at[here, part],
                (2 * chip + core, p, lane),
            )
            if start:
                copy.start()
            else:
                copy.wait_send()

    for e in range(half):
        theirs = 2 * lax.rem(p // 2 + e, half) + 1 - core
        mine = 2 * lax.rem(p // 2 + e, half) + core
        heads_wait(theirs)
        for part in range(parts):

            @pl.loop(0, G // parts)
            def _(b):
                at = pl.ds(pl.multiple_of(b * rows, 128), rows)
                value = features(theirs, part * (G // parts) + b)
                pair_send[e, part, :, at] = value.astype(jnp.bfloat16)

            b_copy(e, part).start()
        heads_wait(mine)
        for part in range(parts):
            b_copy(e, part).wait_recv()

            @pl.loop(0, G // parts)
            def _(b):
                at = pl.ds(pl.multiple_of(b * rows, 128), rows)
                value = features(mine, part * (G // parts) + b)
                value += pair_recv[e, part, :, at].astype(jnp.float32)
                red_send[e, part, :, :, at] = value.astype(jnp.bfloat16).reshape(
                    L, seq // L, rows
                )

            for dl in range(L):
                r_copy(e, part, dl, True)

    def z_copy(q, part, d):
        return remote(
            z_send.at[part, q],
            z_recv.at[part, p],
            z_ssem.at[part, d],
            z_rsem.at[part, p],
            at_plane(q),
        )

    for part in range(parts):
        summed = red_send[lax.rem(pair + 2 * half - core - p // 2, half), part, l].astype(
            jnp.float32
        )
        for sec, lane in others:
            src = (sec // 2) * L + lane
            remote(
                red_send.at[0, part, l],
                red_recv.at[src, part],
                r_ssem.at[0, part, 0],
                r_rsem.at[src, part],
                (sec, p, lane),
            ).wait_recv()
            summed += red_recv[src, part].astype(jnp.float32)
        z_send[part] = summed.astype(jnp.bfloat16).reshape(NP, tokens, G * rows // parts)
        for d in range(1, NP):
            z_copy(lax.rem(p + d, NP), part, d).start()
        z_recv[part, p] = z_send[part, p]
    for part in range(parts):
        for d in range(1, NP):
            q = lax.rem(p + d, NP)
            remote(
                z_send.at[part, q],
                z_recv.at[part, q],
                z_ssem.at[part, d],
                z_rsem.at[part, q],
                at_plane(q),
            ).wait_recv()
    for c in range(S * NP):
        out[:, c * strip : (c + 1) * strip] = z_recv[c // NP, c % NP]

    for d in range(1, NP):
        q = lax.rem(p + d, NP)
        x_copy(q, p, d).wait_send()
        part_copy(pa_send, pa_recv, pa_ssem, pa_rsem, d).wait_send()
        part_copy(pb_send, pb_recv, pb_ssem, pb_rsem, d).wait_send()
        head_copy(heads_a, ha_ssem, ha_rsem, d).wait_send()
        head_copy(heads_b, hb_ssem, hb_rsem, d).wait_send()
        for part in range(parts):
            z_copy(q, part, d).wait_send()
    for i in range(1, G):
        a_copy(i).wait_send()
        w_copy(i).wait_send()
        o_copy(i).wait_send()
    g_copy(j, g_ssem.at[0], to_lane).wait_send()
    g_copy(j, g_ssem.at[1], to_section).wait_send()
    corner_copy(section_block, 0, to_lane).wait_send()
    corner_copy(lane_block, 1, to_section).wait_send()
    for n, (sec, lane) in enumerate(same_core):
        g_copy(sec * L + lane, f_ssem.at[n], (sibling, p, l)).wait_send()
    k_copy(core).wait_send()
    for e in range(half):
        for part in range(parts):
            b_copy(e, part).wait_send()
            for dl in range(L):
                r_copy(e, part, dl, False)


def fused(hidden, norm_gain, lengths, *weights):
    S, NP, L = (lax.axis_size(a) for a in ("section", "plane", "lane"))
    G = S * L
    half = S // 2
    rows = weights[0].shape[0]
    hc = weights[0].shape[1] // G
    first = hc // 2
    split = hc - first
    width = first + HEAD_DIMENSION
    tokens = hidden.shape[1]
    seq = tokens * NP * L
    order = np.arange(seq).reshape(NP, L, tokens).transpose(1, 0, 2).reshape(seq)
    cosine, sine = rope_tables(order)
    bf, f32 = jnp.bfloat16, jnp.float32
    dma = pltpu.SemaphoreType.DMA
    vmem = pl.BlockSpec(memory_space=pltpu.VMEM)
    hbm = pl.BlockSpec(memory_space=pl.ANY)
    smem = pl.BlockSpec(memory_space=pltpu.SMEM)
    scratch = [
        pltpu.VMEM((2, 4, rows, max(width, hc)), f32),
        pltpu.VMEM((G, rows, width), bf),
        pltpu.VMEM((G, rows, width), bf),
        pltpu.VMEM((G, rows, split), bf),
        pltpu.VMEM((G, rows, split), bf),
        pltpu.VMEM((G, rows, hc), bf),
        pltpu.VMEM((G, rows, hc), bf),
        pltpu.VMEM((NP, tokens, G * rows), bf),
        pltpu.VMEM((G, NP, tokens, G * rows), bf),
        pltpu.VMEM((NP - 1, seq, width), bf),
        pltpu.VMEM((NP, seq, width), bf),
        pltpu.VMEM((NP - 1, seq, split), bf),
        pltpu.VMEM((NP, seq, split), bf),
        pltpu.VMEM((seq, width), f32),
        pltpu.VMEM((seq, split), f32),
        pltpu.VMEM((2, seq, HEAD_DIMENSION), bf),
        pltpu.VMEM((NP, seq, first), bf),
        pltpu.VMEM((NP, seq, split), bf),
        pltpu.VMEM((half, S, seq, L * rows), bf),
        pltpu.VMEM((half, S, seq, L * rows), bf),
        pltpu.VMEM((half, S, L, seq // L, L * rows), bf),
        pltpu.VMEM((half * L, S, seq // L, L * rows), bf),
        pltpu.VMEM((S, NP, tokens, L * rows), bf),
        pltpu.VMEM((S, NP, tokens, L * rows), bf),
        pltpu.VMEM((8, 128), jnp.int32),
        pltpu.VMEM((8, 128), jnp.int32),
        dma((2, 4, 2)),
        dma((4,)),
    ]
    scratch += [dma((G,))] * 6
    scratch += [dma((NP,))] * 2
    scratch += [dma((half * L,)), dma((G,)), dma((2,)), dma((2,)), dma((half * L,))]
    scratch += [dma((NP,))] * 4
    scratch += [dma, dma]
    scratch += [dma((NP,))] * 4
    scratch += [dma((half, S))] * 2
    scratch += [dma((half, S, L)), dma((half * L, S))]
    scratch += [dma((S, NP))] * 2
    scratch += [dma((S,)), dma]
    result = pl.pallas_call(
        functools.partial(block_kernel, (S, NP, L)),
        out_shape=jax.ShapeDtypeStruct(hidden.shape[1:], bf),
        in_specs=[vmem, vmem, smem, vmem, vmem] + [hbm] * 12,
        out_specs=vmem,
        scratch_shapes=scratch,
        compiler_params=pltpu.CompilerParams(
            collective_id=0, has_side_effects=True, vmem_limit_bytes=58 * 2**20
        ),
        cost_estimate=pl.CostEstimate(
            flops=8 * 10**9, bytes_accessed=4 * 10**7, transcendentals=10**6
        ),
    )(
        hidden[0],
        norm_gain[None, :],
        lengths,
        jnp.asarray(cosine),
        jnp.asarray(sine),
        *weights,
    )
    return result[None]


def layer(hidden, norm_gain, lengths, *weights):
    whole_tiles = (
        hidden.shape[1] % 16 == 0
        and weights[0].shape[0] % 128 == 0
        and lax.axis_size("section") % 2 == 0
        and lax.axis_size("section") * lax.axis_size("lane") == 2 * KEYVAL_HEADS
        and lax.axis_size("section") == 2 * lax.axis_size("lane")
        and lax.axis_size("plane") % 2 == 0
        and weights[0].shape[1] % (4 * HEAD_DIMENSION * KEYVAL_HEADS) == 0
    )
    return (fused if whole_tiles else on_device)(hidden, norm_gain, lengths, *weights)


def solution(mesh):
    sections, tensors = mesh.shape["section"], mesh.shape["tensor"]
    lanes = tensors // sections
    grid = Mesh(
        mesh.devices.reshape(sections, tensors // lanes, lanes), ("section", "plane", "lane")
    )
    row_spec = P(("section", "plane", "lane"), None)
    token_spec = P("section", ("plane", "lane"), None)
    return jax.shard_map(
        layer,
        mesh=grid,
        in_specs=(token_spec, P(), P("section")) + (row_spec,) * 12,
        out_specs=token_spec,
        check_vma=False,
    )
```
